32 devices in a mesh: tm: 4 (over y, core), vert: 8 (over z, x).
Axes of the slice: x: 2, y: 2, z: 4, core: 2. Of those that a mesh axis runs over, the one named last changes fastest.
Arguments:
- features: bfloat16 [32, 4096, 128], P('tm', 'vert'), may hold values from -6 to 6
- tile_cols: int32 [32, 32, 8], P('tm', 'vert'), may hold values from 0 to 31, as said below
- tile_vals: bfloat16 [32, 32, 8, 128, 128], P('tm', 'vert'), may hold values from -0.1875 to 0.1875
- space_weight: bfloat16 [128, 128], replicated, may hold values from -0.5 to 0.5
- positions: bfloat16 [32, 128], replicated, may hold values from -6 to 6
- attn_proj: bfloat16 [128, 384], replicated, may hold values from -0.5 to 0.5
- attn_out: bfloat16 [128, 128], replicated, may hold values from -0.5 to 0.5
- norm_gain: float32 [128], replicated, may hold values from 0.1 to 1.9
- mlp_up: bfloat16 [128, 512], replicated, may hold values from -0.5 to 0.5
- mlp_down: bfloat16 [512, 128], replicated, may hold values from -0.25 to 0.25
Outputs:
- embedded: bfloat16 [32, 4096, 128], P('tm', 'vert')
The draws below stay inside these ranges and needn't reach their ends.
Inputs may be any that keep to these rules, and one draw needn't show every extreme that they name: `tile_cols`: for each snapshot and each group of 4 consecutive row blocks, the listed column blocks name at most two distinct blocks among those of any one group (blocks c with the same c // 4), and exactly two for some group.
All inputs are finite; a program needn't handle non-finite values.
Results may differ from the reference program's by a relative error of at most 0.0064.
Values may be sent and summed in bfloat16 or wider, within the bound.
No kernel may reach another device: no remote copies, remote signals or barrier semaphores. Data moves between devices by JAX's collectives and lax.ppermute only.
A program may use at most 128 MiB of HBM per device.

```python
import math
import jax
import jax.numpy as jnp
from jax import lax

D = 128
HEADS = 16
FFN = 512
TB = 128
TILES = 8
SNAPS = 32
BLK_DEV = 4
NBLK = 32
VERTS = 4096
VT = 128
N_VERT = 8


def draw_tile_cols(key, part):
    key_first, key_second, key_owner, key_slot = jax.random.split(jax.random.fold_in(key, 11), 4)
    first = jax.random.randint(key_first, (SNAPS, N_VERT, N_VERT), 0, BLK_DEV, dtype=jnp.int32)
    second = (first + jax.random.randint(key_second, (SNAPS, N_VERT, N_VERT), 1, BLK_DEV, dtype=jnp.int32)) % BLK_DEV
    choices_all = jnp.stack([first, second], axis=-1).reshape(SNAPS, N_VERT, N_VERT * 2)
    owners = jax.random.randint(key_owner, (SNAPS, N_VERT, BLK_DEV * TILES), 0, N_VERT, dtype=jnp.int32)
    slots = jax.random.randint(key_slot, (SNAPS, N_VERT, BLK_DEV * TILES), 0, 2, dtype=jnp.int32)
    owners = owners.at[:, :, 0].set(0).at[:, :, 1].set(0)
    slots = slots.at[:, :, 0].set(0).at[:, :, 1].set(1)
    local_blk = jnp.take_along_axis(choices_all, owners * 2 + slots, axis=2)
    columns = owners * BLK_DEV + local_blk
    return columns.reshape(SNAPS, N_VERT * BLK_DEV, TILES).astype(jnp.int32)


def level_of(rng, dims, cuts, least, high):
    def one(position, blocks):
        draws = jax.random.uniform(jax.random.fold_in(jax.random.fold_in(rng, 6), position), (blocks,), jnp.float32, least / len(cuts), high / len(cuts))
        return jnp.repeat(jnp.exp(draws), dims[position] // blocks).reshape((-1,) + (1,) * (len(dims) - position - 1))

    factor_of = one(*cuts[0])
    for cut in cuts[1:]:
        factor_of = factor_of * one(*cut)
    return factor_of


def noise(key, dims, scale, limit, shards=(), held_as=jnp.bfloat16):
    level = level_of(key, dims, shards, -0.22, 0.18) if shards else 1.0
    drawn = jax.random.normal(key, dims, jnp.float32) * scale * level
    return jnp.minimum(jnp.maximum(drawn, -limit), limit).astype(held_as)


def setup_inputs(seed: int = 0) -> dict:
    key_list = jax.random.split(jax.random.key(seed), 11)
    features = noise(key_list[0], (SNAPS, VERTS, D), 1.0, 6.0, ((0, 4), (1, 8)))
    tile_cols = draw_tile_cols(jax.random.fold_in(key_list[10], 71), 0)
    tile_vals = noise(key_list[2], (SNAPS, NBLK, TILES, TB, TB), (TILES * TB) ** -0.5, 0.1875, ((0, 4), (1, 8)))
    space_weight = noise(key_list[3], (D, D), D ** -0.5, 0.5)
    positions = noise(key_list[4], (SNAPS, D), 1.0, 6.0)
    attn_proj = noise(key_list[5], (D, 3 * D), D ** -0.5, 0.5)
    attn_out = noise(key_list[6], (D, D), D ** -0.5, 0.5)
    norm_gain = jnp.clip(1.0 + 0.18 * jax.random.normal(key_list[7], (D,), jnp.float32), 0.1, 1.9)
    mlp_up = noise(key_list[8], (D, FFN), D ** -0.5, 0.5)
    mlp_down = noise(key_list[9], (FFN, D), FFN ** -0.5, 0.25)
    return dict(features=features, tile_cols=tile_cols, tile_vals=tile_vals, space_weight=space_weight, positions=positions, attn_proj=attn_proj, attn_out=attn_out, norm_gain=norm_gain, mlp_up=mlp_up, mlp_down=mlp_down)


cap_value = 4.0
norm_eps = 1e-05

def spatial_snap(feature_snap, cols_snap, vals_snap, space_weight):
    grouped = feature_snap.reshape(NBLK, TB, D)
    blocks = jnp.take(grouped, cols_snap.reshape(-1), axis=0).reshape(NBLK, TILES, TB, D)
    summed = jnp.einsum('rkij,rkjd->rid', vals_snap.astype(jnp.float32), blocks.astype(jnp.float32)).astype(jnp.bfloat16)
    hidden = jax.nn.relu(jnp.dot(summed.reshape(-1, D), space_weight, preferred_element_type=jnp.float32))
    return hidden.astype(jnp.bfloat16).reshape(VERTS, D)

def temporal(hidden, positions, attn_proj, attn_out, norm_gain, mlp_up, mlp_down):
    snap_total = hidden.shape[0]
    head_dim = D // HEADS
    mixed_in = (hidden.astype(jnp.float32) + positions.astype(jnp.float32)[:, None, :]).astype(jnp.bfloat16)
    flat_in = mixed_in.reshape(-1, D)
    projected = jnp.dot(flat_in, attn_proj, preferred_element_type=jnp.float32).astype(jnp.bfloat16)
    projected = projected.reshape(snap_total, -1, 3, HEADS, head_dim)
    query_part = projected[:, :, 0].astype(jnp.float32)
    key_part = projected[:, :, 1].astype(jnp.float32)
    value_part = projected[:, :, 2].astype(jnp.float32)
    scores = jnp.einsum('tvhd,uvhd->vhtu', query_part, key_part) / math.sqrt(head_dim)
    capped = cap_value * jnp.tanh(scores / cap_value)
    causal = jnp.arange(snap_total)[:, None] >= jnp.arange(snap_total)[None, :]
    raised = jnp.where(causal, jnp.exp(capped), 0.0)
    weights = (raised / lax.optimization_barrier(jnp.sum(raised, axis=-1, keepdims=True))).astype(jnp.bfloat16)
    attended = jnp.einsum('vhtu,uvhd->tvhd', weights.astype(jnp.float32), value_part).astype(jnp.bfloat16)
    stream = flat_in.astype(jnp.float32) + jnp.dot(attended.reshape(-1, D), attn_out, preferred_element_type=jnp.float32)
    centre = lax.optimization_barrier(jnp.mean(stream, axis=-1, keepdims=True))
    spread = lax.optimization_barrier(jnp.mean((stream - centre) ** 2, axis=-1, keepdims=True))
    normed = ((stream - centre) * lax.rsqrt(spread + norm_eps) * norm_gain).astype(jnp.bfloat16)
    expanded = jax.nn.relu(jnp.dot(normed, mlp_up, preferred_element_type=jnp.float32)).astype(jnp.bfloat16)
    output = stream + jnp.dot(expanded, mlp_down, preferred_element_type=jnp.float32)
    return output.astype(jnp.bfloat16).reshape(snap_total, -1, D)

def reference(features, tile_cols, tile_vals, space_weight, positions, attn_proj, attn_out, norm_gain, mlp_up, mlp_down):
    hidden = lax.map(lambda item: spatial_snap(item[0], item[1], item[2], space_weight), (features, tile_cols, tile_vals))
    groups = VERTS // VT
    split_up = hidden.reshape(SNAPS, groups, VT, D).transpose(1, 0, 2, 3)
    result = lax.map(lambda piece: temporal(piece, positions, attn_proj, attn_out, norm_gain, mlp_up, mlp_down), split_up)
    return result.transpose(1, 0, 2, 3).reshape(SNAPS, VERTS, D)
```

```python
import functools
import math

import jax
import jax.numpy as jnp
from jax import lax
from jax.experimental import pallas as pl
from jax.experimental.pallas import tpu as pltpu
from jax.sharding import PartitionSpec as P

HEADS = 16
CAP = 4.0
EPS = 1e-05
VMEM = 56 * 1024 * 1024
BF16 = jnp.bfloat16
F32 = jnp.float32


def split_axis(count):
    inner = 1
    while (inner * 2) * (inner * 2) <= count and count % (inner * 2) == 0:
        inner *= 2
    return count // inner, inner


def dot(a, b):
    return jnp.dot(a, b, preferred_element_type=F32)


def pick_kernel(count, picks, idx_ref, *refs):
    srcs, outs = refs[:count], refs[count:]
    s = pl.program_id(0)
    per_dst = picks
    for d, out in enumerate(outs):
        for j in range(per_dst):
            src = srcs[j // 2]
            out[0, j] = src[0, idx_ref[d, s, j]]


def pick(srcs, idx):
    dsts, snaps, picks = idx.shape
    _, blocks, size, width = srcs[0].shape
    return pl.pallas_call(
        functools.partial(pick_kernel, len(srcs), picks),
        grid_spec=pltpu.PrefetchScalarGridSpec(
            num_scalar_prefetch=1,
            grid=(snaps,),
            in_specs=[pl.BlockSpec((1, blocks, size, width), lambda s, i: (s, 0, 0, 0))] * len(srcs),
            out_specs=[pl.BlockSpec((1, picks, size, width), lambda s, i: (s, 0, 0, 0))] * dsts,
        ),
        out_shape=[jax.ShapeDtypeStruct((snaps, picks, size, width), BF16)] * dsts,
        name="pick_blocks",
    )(idx, *srcs)


def spatial_kernel(count, slot_ref, vals_ref, weight_ref, pos_ref, *refs):
    srcs, out, held = refs[:count], refs[count], refs[count + 1]
    s = pl.program_id(0)
    base = 0
    for src in srcs:
        held[base : base + src.shape[1]] = src[0]
        base += src.shape[1]
    rows, tiles, size, _ = vals_ref.shape[1:]
    position = jnp.broadcast_to(pos_ref[pl.ds(s, 1), :], (size, pos_ref.shape[1])).T
    for r in range(rows):
        left = jnp.concatenate([vals_ref[0, r, k] for k in range(tiles)], axis=1)
        right = jnp.concatenate([held[slot_ref[s, r * tiles + k]] for k in range(tiles)], axis=0)
        summed = dot(left, right).astype(BF16)
        hidden = lax.dot_general(
            weight_ref[...], summed, (((1,), (1,)), ((), ())), preferred_element_type=F32
        )
        hidden = jnp.maximum(hidden, 0.0).astype(BF16).astype(F32)
        out[0, :, r * size : (r + 1) * size] = (hidden + position).astype(BF16)


def spatial(slots, vals, weight_t, pos, srcs):
    snaps, rows, tiles, size, _ = vals.shape
    width = weight_t.shape[0]
    held = sum(a.shape[1] for a in srcs)
    block = lambda a: pl.BlockSpec((1,) + a.shape[1:], lambda s, i: (s,) + (0,) * (a.ndim - 1))
    whole = lambda a: pl.BlockSpec(a.shape, lambda s, i: (0,) * a.ndim)
    return pl.pallas_call(
        functools.partial(spatial_kernel, len(srcs)),
        grid_spec=pltpu.PrefetchScalarGridSpec(
            num_scalar_prefetch=1,
            grid=(snaps,),
            in_specs=[block(vals), whole(weight_t), whole(pos)] + [block(a) for a in srcs],
            out_specs=pl.BlockSpec((1, width, rows * size), lambda s, i: (s, 0, 0)),
            scratch_shapes=[pltpu.VMEM((held, size, width), BF16)],
        ),
        out_shape=jax.ShapeDtypeStruct((snaps, width, rows * size), BF16),
        compiler_params=pltpu.CompilerParams(vmem_limit_bytes=VMEM),
        name="spatial",
    )(slots, vals, weight_t, pos, *srcs)


def temporal_kernel(
    others, me_ref, qkv_ref, proj_ref, gain_ref, up_ref, down_ref, own_ref, *refs
):
    other_refs, out_ref = refs[:others], refs[others]
    q_s, k_s, v_s, att_s = refs[others + 1 :]
    snaps, width, lanes = own_ref.shape
    head_dim = width // HEADS
    me = me_ref[0]
    scale = 1.0 / (CAP * math.sqrt(head_dim))

    def project(ref, base, rows_from):
        for s in range(0, snaps, 2):
            two = jnp.concatenate([ref[s], ref[s + 1]], axis=1)
            got = dot(qkv_ref[rows_from:, :], two).astype(BF16).astype(F32)
            for i in range(2):
                half = got[:, i * lanes : (i + 1) * lanes]
                if rows_from == 0:
                    q_s[s + i] = half[:width] * scale
                k_s[base + s + i] = half[width - rows_from : 2 * width - rows_from]
                v_s[base + s + i] = half[2 * width - rows_from :]

    project(own_ref, 0, 0)
    for i, ref in enumerate(other_refs):

        @pl.when((me ^ (i + 1)) < me)
        def _(i=i, ref=ref):
            project(ref, (i + 1) * snaps, width)

    def pair(q, u, carry):
        total, acc = carry
        k = k_s[u].reshape(head_dim, HEADS, lanes)
        v = v_s[u].reshape(head_dim, HEADS, lanes)
        raw = q[0] * k[0]
        for d in range(1, head_dim):
            raw = raw + q[d] * k[d]
        e = jnp.exp(CAP * jnp.tanh(raw))
        return total + e, tuple(acc[d] + e * v[d] for d in range(head_dim))

    for t in range(snaps):
        q3 = q_s[t].reshape(head_dim, HEADS, lanes)
        q = tuple(q3[d] for d in range(head_dim))
        zero = jnp.zeros((HEADS, lanes), F32)
        carry = (zero, (zero,) * head_dim)
        for u in range(t + 1):
            carry = pair(q, u, carry)
        for i in range(others):
            base = (i + 1) * snaps
            steps = jnp.where((me ^ (i + 1)) < me, snaps // 4, 0)

            def four(n, c, base=base):
                for j in range(4):
                    c = pair(q, base + n * 4 + j, c)
                return c

            carry = lax.fori_loop(0, steps, four, carry)
        total, acc = carry
        inv = 1.0 / total
        att_s[t] = jnp.concatenate([acc[d] * inv for d in range(head_dim)], axis=0).astype(BF16)

    for s in range(0, snaps, 2):
        two = jnp.concatenate([own_ref[s], own_ref[s + 1]], axis=1).astype(F32)
        att = jnp.concatenate([att_s[s], att_s[s + 1]], axis=1)
        stream = two + dot(proj_ref[...], att)
        centre = jnp.mean(stream, axis=0, keepdims=True)
        away = stream - centre
        spread = jnp.mean(away * away, axis=0, keepdims=True)
        gain = jnp.concatenate([gain_ref[...]] * 2, axis=1)
        normed = (away * lax.rsqrt(spread + EPS) * gain).astype(BF16)
        expanded = jnp.maximum(dot(up_ref[...], normed), 0.0).astype(BF16)
        final = stream + dot(down_ref[...], expanded)
        for i in range(2):
            out_ref[s + i] = final[:, i * lanes : (i + 1) * lanes].T.astype(BF16)


def temporal(me, qkv_t, proj_t, gain, up_t, down_t, own, others):
    snaps, width, verts = own.shape
    lanes = 128
    whole = lambda a: pl.BlockSpec(a.shape, lambda g, i: (0,) * a.ndim)
    part = pl.BlockSpec((snaps, width, lanes), lambda g, i: (0, 0, g))
    total = snaps * (len(others) + 1)
    return pl.pallas_call(
        functools.partial(temporal_kernel, len(others)),
        grid_spec=pltpu.PrefetchScalarGridSpec(
            num_scalar_prefetch=1,
            grid=(verts // lanes,),
            in_specs=[whole(a) for a in (qkv_t, proj_t, gain, up_t, down_t)]
            + [part] * (1 + len(others)),
            out_specs=pl.BlockSpec((snaps, lanes, width), lambda g, i: (0, g, 0)),
            scratch_shapes=[
                pltpu.VMEM((snaps, width, lanes), F32),
                pltpu.VMEM((total, width, lanes), F32),
                pltpu.VMEM((total, width, lanes), F32),
                pltpu.VMEM((snaps, width, lanes), BF16),
            ],
        ),
        out_shape=jax.ShapeDtypeStruct((snaps, verts, width), BF16),
        compiler_params=pltpu.CompilerParams(vmem_limit_bytes=VMEM),
        name="temporal",
    )(me, qkv_t, proj_t, gain, up_t, down_t, own, *others)


def local(
    features,
    tile_cols,
    tile_vals,
    space_weight,
    positions,
    attn_proj,
    attn_out,
    norm_gain,
    mlp_up,
    mlp_down,
):
    snaps, verts, width = features.shape
    rows, tiles, size = tile_vals.shape[1:4]
    head_dim = width // HEADS
    times = lax.axis_size("tm")
    count = lax.axis_size("vert")
    outer, inner = split_axis(count)
    me_t = lax.axis_index("tm")
    me_v = lax.axis_index("vert")
    me_o, me_i = me_v // inner, me_v % inner
    blocks = features.reshape(snaps, rows, size, width)

    all_cols = lax.all_gather(tile_cols.reshape(snaps, rows * tiles), "vert", axis=0)
    owner = all_cols // rows
    loc = all_cols % rows
    hit = owner[..., None] == jnp.arange(count, dtype=jnp.int32)
    low = jnp.min(jnp.where(hit, loc[..., None], rows - 1), axis=2)
    high = jnp.max(jnp.where(hit, loc[..., None], 0), axis=2)
    wanted = jnp.stack([low, high], axis=-1)

    cols = tile_cols.reshape(snaps, rows * tiles)
    col_owner, col_loc = cols // rows, cols % rows
    col_o, col_i = col_owner // inner, col_owner % inner
    my_hit = col_owner[..., None] == jnp.arange(count, dtype=jnp.int32)
    my_low = jnp.min(jnp.where(my_hit, col_loc[..., None], rows - 1), axis=1)
    slot_low = jnp.sum(jnp.where(my_hit, my_low[:, None, :], 0), axis=2)
    second = (col_loc != slot_low).astype(jnp.int32)
    near = (col_i ^ me_i) * rows + col_loc
    far = inner * rows + ((col_o ^ me_o) - 1) * (2 * inner) + (col_i ^ me_i) * 2 + second
    slots = jnp.where(col_o == me_o, near, far)

    def send_inner(a, k):
        return lax.ppermute(a, "vert", [(v, v ^ k) for v in range(count)])

    def send_outer(a, k):
        return lax.ppermute(a, "vert", [(v, v ^ (k * inner)) for v in range(count)])

    idx = []
    for k in range(1, outer):
        want = wanted[me_v ^ (k * inner)]
        mine = [want[:, me_v ^ j] for j in range(inner)]
        idx.append(jnp.concatenate(mine, axis=-1))
    idx = jnp.stack(idx)

    layer = [blocks] + [send_inner(blocks, j) for j in range(1, inner)]
    picked = pick(layer, idx)
    arrived = [send_outer(picked[k - 1], k) for k in range(1, outer)]

    pos = lax.dynamic_slice_in_dim(positions, me_t * snaps, snaps, 0).astype(F32)
    mixed = spatial(slots, tile_vals, space_weight.T, pos, layer + arrived)

    others = [
        lax.ppermute(mixed, "tm", [(m, m ^ k) for m in range(times) if m < (m ^ k)])
        for k in range(1, times)
    ]

    by_head = lambda w: w.reshape(width, HEADS, head_dim).transpose(2, 1, 0).reshape(width, width)
    qkv_t = jnp.concatenate(
        [by_head(attn_proj[:, i * width : (i + 1) * width]) for i in range(3)], axis=0
    )
    proj_t = attn_out.reshape(HEADS, head_dim, width).transpose(2, 1, 0).reshape(width, width)
    gain = jnp.broadcast_to(norm_gain[:, None], (width, 128))
    me = me_t.astype(jnp.int32).reshape(1)
    return temporal(me, qkv_t, proj_t, gain, mlp_up.T, mlp_down.T, mixed, others)


def solution(mesh):
    placed = (
        P("tm", "vert", None),
        P("tm", "vert", None),
        P("tm", "vert", None, None, None),
        P(),
        P(),
        P(),
        P(),
        P(),
        P(),
        P(),
    )
    return jax.shard_map(
        local, mesh=mesh, in_specs=placed, out_specs=P("tm", "vert", None), check_vma=False
    )
```

```python
import functools
import math

import jax
import jax.numpy as jnp
from jax import lax
from jax.experimental import pallas as pl
from jax.experimental.pallas import tpu as pltpu
from jax.sharding import PartitionSpec as P

HEADS = 16
CAP = 4.0
EPS = 1e-05
VMEM = 56 * 1024 * 1024
BF16 = jnp.bfloat16
F32 = jnp.float32
after = lax.optimization_barrier


def split_axis(count):
    inner = 1
    while (inner * 2) * (inner * 2) <= count and count % (inner * 2) == 0:
        inner *= 2
    return count // inner, inner


def dot(a, b):
    return jnp.dot(a, b, preferred_element_type=F32)


def dot_nt(a, b):
    return lax.dot_general(a, b, (((1,), (1,)), ((), ())), preferred_element_type=F32)


def whole(a):
    return pl.BlockSpec(a.shape, lambda *i: (0,) * len(a.shape))


def cost(us):
    return pl.CostEstimate(flops=int(us * 1.15e9), bytes_accessed=1024, transcendentals=0)


def prepare_kernel(rows, count, inner, forward, at_ref, *refs):
    cols_ref, pos_ref, qkv_ref, proj_ref, gain_ref, up_ref, down_ref, space_ref = refs[:8]
    want_o, slot_o, pos_o, qkv_o, proj_o, gain_o, up_o, down_o, space_o, pos_s = refs[8:]
    me = at_ref[0]
    cols = cols_ref[...]
    rel = (cols // rows) ^ me
    loc = cols % rows
    slots = jnp.zeros_like(cols)
    for k in range(count):
        hit = rel == k
        least = lambda a: jnp.min(jnp.min(a, axis=2, keepdims=True), axis=1, keepdims=True)
        low = least(jnp.where(hit, loc, rows - 1))
        high = -least(jnp.where(hit, -loc, 0))
        want_o[:, :, 2 * k : 2 * k + 1] = low
        want_o[:, :, 2 * k + 1 : 2 * k + 2] = high
        second = jnp.where(loc == low, 0, 1)
        if forward:
            o = me // inner
            middle = jnp.where((o == 1) | (o == 2), 1, 0)
            half = (k // 2 - 2) * 2
            if k in (0, 2):
                at = (k // 2) * rows + loc
            elif k in (1, 3):
                at = 4 * rows + (k // 2) * 2 + second
            elif k % 2 == 0:
                at = jnp.where(middle == 1, (3 if k == 4 else 2) * rows + loc, 6 * rows + half + second)
            else:
                at = (7 - 2 * middle) * rows + half + second
        elif k < inner:
            at = k * rows + loc
        else:
            at = inner * rows + (k - inner) * 2 + second
        slots = jnp.where(hit, at, slots)
    slot_o[...] = slots

    width = proj_ref.shape[0]
    head_dim = width // HEADS
    snaps = pos_o.shape[0]
    pos_s[...] = pos_ref[...].astype(F32)
    pos_o[...] = pos_s[pl.ds(at_ref[1] * snaps, snaps), :]
    to = lax.broadcasted_iota(jnp.int32, (width, width), 0)
    source = lax.broadcasted_iota(jnp.int32, (width, width), 1)
    by_head = jnp.where((to % HEADS) * head_dim + to // HEADS == source, 1.0, 0.0).astype(BF16)
    for i in range(3):
        part = slice(i * width, (i + 1) * width)
        qkv_o[part, :] = dot_nt(by_head, qkv_ref[:, part]).astype(BF16)
    flip = lambda a: a.astype(F32).T.astype(BF16)
    proj_o[...] = dot_nt(flip(proj_ref[...]), by_head).astype(BF16)
    gain_o[...] = jnp.broadcast_to(gain_ref[...], gain_o.shape).T
    for i in range(up_ref.shape[1] // width):
        part = slice(i * width, (i + 1) * width)
        up_o[part, :] = flip(up_ref[:, part])
        down_o[:, part] = flip(down_ref[part, :])
    space_o[...] = flip(space_ref[...])


def prepare(at, cols, positions, weights, rows, count, inner, forward):
    snaps = cols.shape[0]
    qkv, proj, gain, up, down, space = weights
    width = proj.shape[0]
    ins = [cols, positions, qkv, proj, gain.reshape(1, width), up, down, space]
    shape = jax.ShapeDtypeStruct
    outs = [
        shape((snaps, 1, 2 * count), jnp.int32),
        shape(cols.shape, jnp.int32),
        shape((snaps, width), F32),
        shape((3 * width, width), BF16),
        shape((width, width), BF16),
        shape((width, width), F32),
        shape((up.shape[1], width), BF16),
        shape((width, down.shape[0]), BF16),
        shape((width, width), BF16),
    ]
    return pl.pallas_call(
        functools.partial(prepare_kernel, rows, count, inner, forward),
        grid_spec=pltpu.PrefetchScalarGridSpec(
            num_scalar_prefetch=1,
            grid=(1,),
            in_specs=[whole(a) for a in ins],
            out_specs=[whole(a) for a in outs],
            scratch_shapes=[pltpu.VMEM(positions.shape, F32)],
        ),
        out_shape=outs,
        compiler_params=pltpu.CompilerParams(vmem_limit_bytes=VMEM),
        name="prepare",
    )(at, *ins)


def pick_kernel(jobs, wants, offsets, *refs):
    outs = refs[len(refs) - len(jobs) :]
    want_refs, srcs = refs[:wants], refs[wants : len(refs) - len(jobs)]
    for (which, pairs, lo, _), out in zip(jobs, outs):
        for s in range(out.shape[0]):
            for j, (src, rel) in enumerate(pairs):
                for i in range(2):
                    block = want_refs[which][lo + s, 0, 2 * rel + i]
                    out[s, 2 * j + i] = srcs[src][lo + s - offsets[src], block]


def pick(srcs, offsets, wants, jobs):
    size, width = srcs[0].shape[2:]
    shapes = [
        jax.ShapeDtypeStruct((hi - lo, 2 * len(pairs), size, width), BF16)
        for _, pairs, lo, hi in jobs
    ]
    return pl.pallas_call(
        functools.partial(pick_kernel, jobs, len(wants), offsets),
        grid_spec=pltpu.PrefetchScalarGridSpec(
            num_scalar_prefetch=len(wants),
            grid=(1,),
            in_specs=[whole(a) for a in srcs],
            out_specs=[whole(a) for a in shapes],
        ),
        out_shape=shapes,
        compiler_params=pltpu.CompilerParams(vmem_limit_bytes=VMEM),
        cost_estimate=cost(3),
        name="pick_blocks",
    )(*wants, *srcs)


def spatial_kernel(start, offsets, slot_ref, vals_ref, weight_ref, pos_ref, *refs):
    srcs, (*outs, held, vals, sums, held_sem, vals_sem) = refs[: len(offsets)], refs[len(offsets) :]
    snaps, rows, tiles, size, _ = vals.shape
    each = rows // len(outs)
    copies, arriving = [], []
    for src, offset in zip(srcs, offsets):
        for first in range(0, src.shape[1], rows):
            unit = len(copies)
            span = slice(start - offset, start - offset + snaps)
            copies.append(
                pltpu.make_async_copy(
                    src.at[span, first : first + rows], held.at[unit], held_sem.at[unit]
                )
            )
    for s in range(snaps):
        arriving.append(pltpu.make_async_copy(vals_ref.at[start + s], vals.at[s], vals_sem.at[s]))
    for copy in arriving[:1] + copies + arriving[1:]:
        copy.start()
    for copy in copies:
        copy.wait()
    for s in range(snaps):
        arriving[s].wait()
        for r in range(rows):
            left = jnp.concatenate([vals[s, r, k] for k in range(tiles)], axis=1)
            right = []
            for k in range(tiles):
                slot = slot_ref[start + s, r, k]
                right.append(held[slot // rows, s, slot % rows])
            summed = dot(left, jnp.concatenate(right, axis=0)).astype(BF16)
            sums[(s * rows + r) * size : (s * rows + r + 1) * size, :] = summed
    for s in range(snaps):
        pos = pos_ref[start + s : start + s + 1, :]
        position = jnp.broadcast_to(pos, (size, pos.shape[1])).T
        some = sums[s * rows * size : (s + 1) * rows * size, :]
        hidden = jnp.maximum(dot_nt(weight_ref[...], some), 0.0).astype(BF16).astype(F32)
        for r in range(rows):
            mixed = hidden[:, r * size : (r + 1) * size] + position
            outs[r // each][r % each, s] = mixed.astype(BF16)


def spatial(slots, vals, start, stop, weight_t, pos, srcs, parts):
    rows, tiles, size, _ = vals.shape[1:]
    snaps = stop - start
    width = weight_t.shape[0]
    units = sum(a.shape[1] for a, _ in srcs) // rows
    anywhere = pl.BlockSpec(memory_space=pl.ANY)
    out = jax.ShapeDtypeStruct((rows // parts, snaps, width, size), BF16)
    return pl.pallas_call(
        functools.partial(spatial_kernel, start, [first for _, first in srcs]),
        grid_spec=pltpu.PrefetchScalarGridSpec(
            num_scalar_prefetch=1,
            grid=(1,),
            in_specs=[anywhere, whole(weight_t), whole(pos)] + [anywhere] * len(srcs),
            out_specs=[whole(out)] * parts,
            scratch_shapes=[
                pltpu.VMEM((units, snaps, rows, size, width), BF16),
                pltpu.VMEM((snaps, rows, tiles, size, size), BF16),
                pltpu.VMEM((snaps * rows * size, width), BF16),
                pltpu.SemaphoreType.DMA((units,)),
                pltpu.SemaphoreType.DMA((snaps,)),
            ],
        ),
        out_shape=[out] * parts,
        compiler_params=pltpu.CompilerParams(vmem_limit_bytes=VMEM),
        cost_estimate=cost(2 * snaps),
        name="spatial",
    )(slots, vals, weight_t, pos, *[a for a, _ in srcs])


def temporal_kernel(sizes, others, me_ref, qkv_ref, proj_ref, gain_ref, up_ref, down_ref, *refs):
    count = 1 + others
    arrays = refs[: count * len(sizes)]
    out_ref, k_s, v_s, q_s, acc_s, total_s, att_s = refs[-7:]
    snaps = sum(sizes)
    width, lanes = arrays[0].shape[2:]
    head_dim = width // HEADS
    me = me_ref[0]
    scale = 1.0 / (CAP * math.sqrt(head_dim))
    steep = CAP * math.log2(math.e)

    def held(i):
        return [arrays[c * count + i][0, s] for c, n in enumerate(sizes) for s in range(n)]

    def project(i):
        skip = 0 if i == 0 else width
        base = (me ^ i) * snaps
        found = held(i)
        for first in range(0, snaps, 4):
            some = found[first : first + 4]
            got = dot(qkv_ref[skip:, :], jnp.concatenate(some, axis=1)).astype(BF16).astype(F32)
            for j in range(len(some)):
                part = got[:, j * lanes : (j + 1) * lanes]
                if i == 0:
                    q_s[first + j] = part[:width] * scale
                k_s[base + first + j] = part[width - skip : 2 * width - skip]
                v_s[base + first + j] = part[2 * width - skip :]

    project(0)
    for i in range(1, count):
        pl.when((me ^ i) < me)(functools.partial(project, i))

    def attend(at, keys, fresh=False):
        q = [q_s[at, d * HEADS : (d + 1) * HEADS] for d in range(head_dim)]
        total, acc = None, None
        for u in keys:
            row = lambda ref, d: ref[u, d * HEADS : (d + 1) * HEADS]
            raw = q[0] * row(k_s, 0)
            for d in range(1, head_dim):
                raw = raw + q[d] * row(k_s, d)
            e = jnp.exp2(steep * jnp.tanh(raw))
            if total is None:
                total, acc = e, [e * row(v_s, d) for d in range(head_dim)]
            else:
                total = total + e
                acc = [acc[d] + e * row(v_s, d) for d in range(head_dim)]
        for d in range(head_dim):
            span = slice(d * HEADS, (d + 1) * HEADS)
            acc_s[at, span] = acc[d] if fresh else acc_s[at, span] + acc[d]
        total_s[at] = total if fresh else total_s[at] + total

    for s in range(snaps):
        attend(s, [me * snaps + j for j in range(s + 1)], fresh=True)

    def earlier(m, none):
        for at in range(snaps):
            attend(at, [m * snaps + j for j in range(snaps)])
        return none

    lax.fori_loop(0, me, earlier, 0)

    mine = held(0)
    for at in range(snaps):
        inv = 1.0 / total_s[at]
        for d in range(head_dim):
            span = slice(d * HEADS, (d + 1) * HEADS)
            att_s[span, at * lanes : (at + 1) * lanes] = (acc_s[at, span] * inv).astype(BF16)
    half = snaps // 2
    for h in range(2):
        span = slice(h * half * lanes, (h + 1) * half * lanes)
        base = jnp.concatenate(mine[h * half : (h + 1) * half], axis=1).astype(F32)
        stream = base + dot(proj_ref[...], att_s[:, span])
        centre = jnp.mean(stream, axis=0, keepdims=True)
        away = stream - centre
        spread = jnp.mean(away * away, axis=0, keepdims=True)
        gain = jnp.concatenate([gain_ref[...]] * half, axis=1)
        normed = (away * lax.rsqrt(spread + EPS) * gain).astype(BF16)
        expanded = jnp.maximum(dot(up_ref[...], normed), 0.0).astype(BF16)
        out = stream + dot(down_ref[...], expanded)
        for i in range(half):
            out_ref[h * half + i] = out[:, i * lanes : (i + 1) * lanes].T.astype(BF16)


def temporal(me, weights, chunks, first, groups, total, so_far):
    width, lanes = chunks[0][0].shape[2:]
    count = len(chunks[0])
    sizes = [chunk[0].shape[1] for chunk in chunks]
    snaps = sum(sizes)

    def part(a):
        at = first if a.shape[0] == total else 0
        return pl.BlockSpec((1,) + a.shape[1:], lambda g, i: (g + at, 0, 0, 0))

    parts = [a for chunk in chunks for a in chunk]
    extra = [] if so_far is None else [so_far]
    return pl.pallas_call(
        functools.partial(temporal_kernel, sizes, count - 1),
        grid_spec=pltpu.PrefetchScalarGridSpec(
            num_scalar_prefetch=1,
            grid=(groups,),
            in_specs=[whole(a) for a in weights]
            + [part(a) for a in parts]
            + [pl.BlockSpec(memory_space=pl.ANY)] * len(extra),
            out_specs=pl.BlockSpec((snaps, lanes, width), lambda g, i: (0, g + first, 0)),
            scratch_shapes=[
                pltpu.VMEM((snaps * count, width, lanes), F32),
                pltpu.VMEM((snaps * count, width, lanes), F32),
                pltpu.VMEM((snaps, width, lanes), F32),
                pltpu.VMEM((snaps, width, lanes), F32),
                pltpu.VMEM((snaps, HEADS, lanes), F32),
                pltpu.VMEM((width, snaps * lanes), BF16),
            ],
        ),
        out_shape=jax.ShapeDtypeStruct((snaps, total * lanes, width), BF16),
        input_output_aliases={1 + len(weights) + len(parts): 0} if extra else {},
        compiler_params=pltpu.CompilerParams(vmem_limit_bytes=VMEM),
        cost_estimate=cost(10),
        name="temporal",
    )(me, *weights, *parts, *extra)


def send(a, k):
    return lax.ppermute(a, "vert", [(v, v ^ k) for v in range(lax.axis_size("vert"))])


def exchange_direct(blocks, want, inner):
    snaps = blocks.shape[0]
    count = lax.axis_size("vert")
    outer = count // inner
    wants = [send(want, k * inner) for k in range(1, outer)]
    layer = [blocks] + [send(blocks, j) for j in range(1, inner)]
    jobs = [
        (k - 1, [(j, k * inner + j) for j in range(inner)], 0, snaps) for k in range(1, outer)
    ]
    picked = pick(layer, [0] * inner, wants, jobs)
    arrived = [send(picked[k - 1], k * inner) for k in range(1, outer)]
    return [(0, snaps, [(a, 0) for a in layer + arrived])]


def exchange_forward(blocks, want):
    snaps = blocks.shape[0]
    layers = lambda pairs, x=0: [(a * 2 + i, b * 2 + (i ^ x)) for a, b in pairs for i in range(2)]
    go = lambda a, pairs, x=0: lax.ppermute(a, "vert", layers(pairs, x))
    cross = [(1, 2), (2, 1)]
    skip = [(0, 2), (3, 1)]
    ends = [(2, 3), (1, 0)]
    back = [(3, 2), (0, 1)]

    cut = snaps // 2
    first, rest = blocks[:cut], blocks[cut:]
    p1, p2, near = go(first, cross), go(first, skip), send(first, 2)
    wants = [send(want, 1), go(want, back), go(want, back, 1)]
    rest, *wants = after((rest, *wants))

    def forward(own, near, p1, p2, lo, hi):
        srcs = [own, near, p1, p2]
        offsets = [0 if a.shape[0] == snaps else lo for a in srcs]
        jobs = [
            (1, [(2, 4), (3, 6)], lo, hi),
            (2, [(2, 5), (3, 7)], lo, hi),
            (0, [(0, 1), (1, 3)], lo, hi),
            (0, [(3, 5), (2, 7)], lo, hi),
        ]
        f0, f1, x1, x2 = pick(srcs, offsets, wants, jobs)
        f0, f1 = go(f0, ends), go(f1, ends, 1)
        x1, x2 = send(x1, 1), go(x2, [(1, 1), (2, 2)], 1)
        return (lo, hi, list(zip(srcs, offsets)) + [(a, lo) for a in (x1, x2, f0, f1)])

    parts = [forward(first, near, p1, p2, 0, cut)]
    q1, q2, far = go(rest, cross), go(rest, skip), send(rest, 2)
    return parts + [forward(rest, far, q1, q2, cut, snaps)]


def gather_times(own):
    times = lax.axis_size("tm")
    got = [own] + [None] * (times - 1)
    for k in range(1, times):
        if k == 1 or k % 2 == 0:
            pairs = [(m, m ^ k) for m in range(times) if m < (m ^ k)]
            got[k] = lax.ppermute(own, "tm", pairs)
    return got


def pass_on(got, late):
    times = lax.axis_size("tm")
    got = list(got)
    for k in range(3, times, 2):
        pairs = [(m, m ^ 1) for m in range(times) if (m ^ (k - 1)) < m]
        got[k - 1], _ = after((got[k - 1], late))
        got[k] = lax.ppermute(got[k - 1], "tm", pairs)
    return got


def local(
    features,
    tile_cols,
    tile_vals,
    space_weight,
    positions,
    attn_proj,
    attn_out,
    norm_gain,
    mlp_up,
    mlp_down,
):
    snaps, verts, width = features.shape
    rows, tiles, size = tile_vals.shape[1:4]
    count = lax.axis_size("vert")
    outer, inner = split_axis(count)
    me_t = lax.axis_index("tm").astype(jnp.int32)
    me_v = lax.axis_index("vert").astype(jnp.int32)
    blocks = features.reshape(snaps, rows, size, width)

    forward = (outer, inner) == (4, 2)
    weights = (attn_proj, attn_out, norm_gain, mlp_up, mlp_down, space_weight)
    want, slots, pos, *weights, space_t = prepare(
        jnp.stack([me_v, me_t]), tile_cols, positions, weights, rows, count, inner, forward
    )
    me = me_t.reshape(1)
    parts = exchange_forward(blocks, want) if forward else exchange_direct(blocks, want, inner)

    started = []
    for start, stop, srcs in parts[:-1]:
        (own,) = spatial(slots, tile_vals, start, stop, space_t, pos, srcs, 1)
        started.append(gather_times(own))
    start, stop, srcs = parts[-1]
    halves = 2 if rows % 2 == 0 else 1
    owns = spatial(slots, tile_vals, start, stop, space_t, pos, srcs, halves)
    done = [pass_on(got, owns[0]) for got in started]
    last = [gather_times(own) for own in owns]
    out = None
    for h, got in enumerate(last):
        chunks = done + [pass_on(got, owns[0])]
        groups = owns[h].shape[0]
        out = temporal(me, weights, chunks, h * groups, groups, rows, out)
    return out


def solution(mesh):
    placed = (
        P("tm", "vert", None),
        P("tm", "vert", None),
        P("tm", "vert", None, None, None),
        P(),
        P(),
        P(),
        P(),
        P(),
        P(),
        P(),
    )
    return jax.shard_map(
        local, mesh=mesh, in_specs=placed, out_specs=P("tm", "vert", None), check_vma=False
    )
```

```python
import functools
import math

import jax
import jax.numpy as jnp
from jax import lax
from jax.experimental import pallas as pl
from jax.experimental.pallas import tpu as pltpu
from jax.sharding import PartitionSpec as P

HEADS = 16
CAP = 4.0
EPS = 1e-05
VMEM = 24 * 1024 * 1024
BF16 = jnp.bfloat16
F32 = jnp.float32
after = lax.optimization_barrier


def split_axis(count):
    inner = 1
    while (inner * 2) * (inner * 2) <= count and count % (inner * 2) == 0:
        inner *= 2
    return count // inner, inner


def dot(a, b):
    return jnp.dot(a, b, preferred_element_type=F32)


def dot_nt(a, b):
    return lax.dot_general(a, b, (((1,), (1,)), ((), ())), preferred_element_type=F32)


def whole(a):
    return pl.BlockSpec(a.shape, lambda *i: (0,) * len(a.shape))


def near(a):
    return pltpu.with_memory_space_constraint(a, pltpu.VMEM)


def cost(us):
    return pl.CostEstimate(flops=int(us * 1.15e9), bytes_accessed=1024, transcendentals=0)


def prepare_kernel(rows, count, inner, forward, at_ref, *refs):
    cols_ref, pos_ref, qkv_ref, proj_ref, gain_ref, up_ref, down_ref, space_ref = refs[:8]
    want_o, slot_o, pos_o, qkv_o, proj_o, gain_o, up_o, down_o, space_o, pos_s = refs[8:]
    me = at_ref[0]
    cols = cols_ref[...]
    rel = (cols // rows) ^ me
    loc = cols % rows
    slots = jnp.zeros_like(cols)
    for k in range(count):
        hit = rel == k
        least = lambda a: jnp.min(jnp.min(a, axis=2, keepdims=True), axis=1, keepdims=True)
        low = least(jnp.where(hit, loc, rows - 1))
        high = -least(jnp.where(hit, -loc, 0))
        want_o[:, :, 2 * k : 2 * k + 1] = low
        want_o[:, :, 2 * k + 1 : 2 * k + 2] = high
        second = jnp.where(loc == low, 0, 1)
        if forward:
            o = me // inner
            middle = jnp.where((o == 1) | (o == 2), 1, 0)
            half = (k // 2 - 2) * 2
            if k in (0, 2):
                at = (k // 2) * rows + loc
            elif k in (1, 3):
                at = 4 * rows + (k // 2) * 2 + second
            elif k % 2 == 0:
                at = jnp.where(middle == 1, (3 if k == 4 else 2) * rows + loc, 6 * rows + half + second)
            else:
                at = (7 - 2 * middle) * rows + half + second
        elif k < inner:
            at = k * rows + loc
        else:
            at = inner * rows + (k - inner) * 2 + second
        slots = jnp.where(hit, at, slots)
    slot_o[...] = slots

    width = proj_ref.shape[0]
    head_dim = width // HEADS
    snaps = pos_o.shape[0]
    pos_s[...] = pos_ref[...].astype(F32)
    pos_o[...] = pos_s[pl.ds(at_ref[1] * snaps, snaps), :]
    to = lax.broadcasted_iota(jnp.int32, (width, width), 0)
    source = lax.broadcasted_iota(jnp.int32, (width, width), 1)
    by_head = jnp.where((to % HEADS) * head_dim + to // HEADS == source, 1.0, 0.0).astype(BF16)
    for i in range(3):
        part = slice(i * width, (i + 1) * width)
        qkv_o[part, :] = dot_nt(by_head, qkv_ref[:, part]).astype(BF16)
    flip = lambda a: a.astype(F32).T.astype(BF16)
    proj_o[...] = dot_nt(flip(proj_ref[...]), by_head).astype(BF16)
    gain_o[...] = jnp.broadcast_to(gain_ref[...], gain_o.shape).T
    for i in range(up_ref.shape[1] // width):
        part = slice(i * width, (i + 1) * width)
        up_o[part, :] = flip(up_ref[:, part])
        down_o[:, part] = flip(down_ref[part, :])
    space_o[...] = flip(space_ref[...])


def prepare(at, cols, positions, weights, rows, count, inner, forward):
    snaps = cols.shape[0]
    qkv, proj, gain, up, down, space = weights
    width = proj.shape[0]
    ins = [cols, positions, qkv, proj, gain.reshape(1, width), up, down, space]
    shape = jax.ShapeDtypeStruct
    outs = [
        shape((snaps, 1, 2 * count), jnp.int32),
        shape(cols.shape, jnp.int32),
        shape((snaps, width), F32),
        shape((3 * width, width), BF16),
        shape((width, width), BF16),
        shape((width, width), F32),
        shape((up.shape[1], width), BF16),
        shape((width, down.shape[0]), BF16),
        shape((width, width), BF16),
    ]
    return pl.pallas_call(
        functools.partial(prepare_kernel, rows, count, inner, forward),
        grid_spec=pltpu.PrefetchScalarGridSpec(
            num_scalar_prefetch=1,
            grid=(1,),
            in_specs=[whole(a) for a in ins],
            out_specs=[whole(a) for a in outs],
            scratch_shapes=[pltpu.VMEM(positions.shape, F32)],
        ),
        out_shape=outs,
        compiler_params=pltpu.CompilerParams(vmem_limit_bytes=VMEM),
        name="prepare",
    )(at, *ins)


def pick_kernel(jobs, wants, offsets, *refs):
    outs = refs[len(refs) - len(jobs) :]
    want_refs, srcs = refs[:wants], refs[wants : len(refs) - len(jobs)]
    for (which, pairs, lo, _), out in zip(jobs, outs):
        for s in range(out.shape[0]):
            for j, (src, rel) in enumerate(pairs):
                for i in range(2):
                    block = want_refs[which][lo + s, 0, 2 * rel + i]
                    out[s, 2 * j + i] = srcs[src][lo + s - offsets[src], block]


def pick(srcs, offsets, wants, jobs):
    size, width = srcs[0].shape[2:]
    shapes = [
        jax.ShapeDtypeStruct((hi - lo, 2 * len(pairs), size, width), BF16)
        for _, pairs, lo, hi in jobs
    ]
    return pl.pallas_call(
        functools.partial(pick_kernel, jobs, len(wants), offsets),
        grid_spec=pltpu.PrefetchScalarGridSpec(
            num_scalar_prefetch=len(wants),
            grid=(1,),
            in_specs=[whole(srcs[0])] + [pl.BlockSpec(memory_space=pltpu.VMEM)] * (len(srcs) - 1),
            out_specs=[whole(a) for a in shapes],
        ),
        out_shape=shapes,
        compiler_params=pltpu.CompilerParams(vmem_limit_bytes=VMEM),
        cost_estimate=cost(3),
        name="pick_blocks",
    )(*wants, srcs[0], *[near(a) for a in srcs[1:]])


def spatial_kernel(start, offsets, slot_ref, vals_ref, weight_ref, pos_ref, *refs):
    srcs, (*outs, held, vals, sums, own_sem, vals_sem) = refs[: len(offsets)], refs[len(offsets) :]
    snaps, rows, tiles, size, _ = vals.shape
    each = rows // len(outs)
    span = slice(start - offsets[0], start - offsets[0] + snaps)
    own = pltpu.make_async_copy(srcs[0].at[span], held.at[0], own_sem)
    own.start()
    arriving = []
    for s in range(snaps):
        arriving.append(pltpu.make_async_copy(vals_ref.at[start + s], vals.at[s], vals_sem.at[s]))
        arriving[s].start()
    unit = 1
    for src, offset in zip(srcs[1:], offsets[1:]):
        for first in range(0, src.shape[1], rows):
            held[unit] = src[start - offset : start - offset + snaps, first : first + rows]
            unit += 1
    own.wait()
    for s in range(snaps):
        arriving[s].wait()
        for r in range(rows):
            left = jnp.concatenate([vals[s, r, k] for k in range(tiles)], axis=1)
            right = []
            for k in range(tiles):
                slot = slot_ref[start + s, r, k]
                right.append(held[slot // rows, s, slot % rows])
            summed = dot(left, jnp.concatenate(right, axis=0)).astype(BF16)
            sums[(s * rows + r) * size : (s * rows + r + 1) * size, :] = summed
    for s in range(snaps):
        pos = pos_ref[start + s : start + s + 1, :]
        position = jnp.broadcast_to(pos, (size, pos.shape[1])).T
        some = sums[s * rows * size : (s + 1) * rows * size, :]
        hidden = jnp.maximum(dot_nt(weight_ref[...], some), 0.0).astype(BF16).astype(F32)
        for r in range(rows):
            mixed = hidden[:, r * size : (r + 1) * size] + position
            outs[r // each][r % each, s] = mixed.astype(BF16)


def spatial(slots, vals, start, stop, weight_t, pos, srcs, parts):
    rows, tiles, size, _ = vals.shape[1:]
    snaps = stop - start
    width = weight_t.shape[0]
    units = sum(a.shape[1] for a, _ in srcs) // rows
    anywhere = pl.BlockSpec(memory_space=pl.ANY)
    out = jax.ShapeDtypeStruct((rows // parts, snaps, width, size), BF16)
    return pl.pallas_call(
        functools.partial(spatial_kernel, start, [first for _, first in srcs]),
        grid_spec=pltpu.PrefetchScalarGridSpec(
            num_scalar_prefetch=1,
            grid=(1,),
            in_specs=[anywhere, whole(weight_t), whole(pos), anywhere]
            + [pl.BlockSpec(memory_space=pltpu.VMEM)] * (len(srcs) - 1),
            out_specs=[whole(out)] * parts,
            scratch_shapes=[
                pltpu.VMEM((units, snaps, rows, size, width), BF16),
                pltpu.VMEM((snaps, rows, tiles, size, size), BF16),
                pltpu.VMEM((snaps * rows * size, width), BF16),
                pltpu.SemaphoreType.DMA,
                pltpu.SemaphoreType.DMA((snaps,)),
            ],
        ),
        out_shape=[out] * parts,
        compiler_params=pltpu.CompilerParams(vmem_limit_bytes=VMEM),
        cost_estimate=cost(2 * snaps),
        name="spatial",
    )(slots, vals, weight_t, pos, srcs[0][0], *[near(a) for a, _ in srcs[1:]])


def temporal_kernel(sizes, others, me_ref, qkv_ref, proj_ref, gain_ref, up_ref, down_ref, *refs):
    count = 1 + others
    arrays = refs[: count * len(sizes)]
    out_ref, k_s, v_s, q_s, acc_s, total_s, att_s = refs[-7:]
    snaps = sum(sizes)
    width, lanes = arrays[0].shape[2:]
    head_dim = width // HEADS
    me = me_ref[0]
    scale = 1.0 / (CAP * math.sqrt(head_dim))
    steep = CAP * math.log2(math.e)

    def held(i):
        return [arrays[c * count + i][0, s] for c, n in enumerate(sizes) for s in range(n)]

    def project(i):
        skip = 0 if i == 0 else width
        base = (me ^ i) * snaps
        found = held(i)
        for first in range(0, snaps, 4):
            some = found[first : first + 4]
            got = dot(qkv_ref[skip:, :], jnp.concatenate(some, axis=1)).astype(BF16).astype(F32)
            for j in range(len(some)):
                part = got[:, j * lanes : (j + 1) * lanes]
                if i == 0:
                    q_s[first + j] = part[:width] * scale
                k_s[base + first + j] = part[width - skip : 2 * width - skip]
                v_s[base + first + j] = part[2 * width - skip :]

    project(0)
    for i in range(1, count):
        pl.when((me ^ i) < me)(functools.partial(project, i))

    def attend(at, keys, fresh=False):
        q = [q_s[at, d * HEADS : (d + 1) * HEADS] for d in range(head_dim)]
        total, acc = None, None
        for u in keys:
            row = lambda ref, d: ref[u, d * HEADS : (d + 1) * HEADS]
            raw = q[0] * row(k_s, 0)
            for d in range(1, head_dim):
                raw = raw + q[d] * row(k_s, d)
            e = jnp.exp2(steep * jnp.tanh(raw))
            if total is None:
                total, acc = e, [e * row(v_s, d) for d in range(head_dim)]
            else:
                total = total + e
                acc = [acc[d] + e * row(v_s, d) for d in range(head_dim)]
        for d in range(head_dim):
            span = slice(d * HEADS, (d + 1) * HEADS)
            acc_s[at, span] = acc[d] if fresh else acc_s[at, span] + acc[d]
        total_s[at] = total if fresh else total_s[at] + total

    for s in range(snaps):
        attend(s, [me * snaps + j for j in range(s + 1)], fresh=True)

    def earlier(m, none):
        for at in range(snaps):
            attend(at, [m * snaps + j for j in range(snaps)])
        return none

    lax.fori_loop(0, me, earlier, 0)

    mine = held(0)
    for at in range(snaps):
        inv = 1.0 / total_s[at]
        for d in range(head_dim):
            span = slice(d * HEADS, (d + 1) * HEADS)
            att_s[span, at * lanes : (at + 1) * lanes] = (acc_s[at, span] * inv).astype(BF16)
    half = snaps // 2
    for h in range(2):
        span = slice(h * half * lanes, (h + 1) * half * lanes)
        base = jnp.concatenate(mine[h * half : (h + 1) * half], axis=1).astype(F32)
        stream = base + dot(proj_ref[...], att_s[:, span])
        centre = jnp.mean(stream, axis=0, keepdims=True)
        away = stream - centre
        spread = jnp.mean(away * away, axis=0, keepdims=True)
        gain = jnp.concatenate([gain_ref[...]] * half, axis=1)
        normed = (away * lax.rsqrt(spread + EPS) * gain).astype(BF16)
        expanded = jnp.maximum(dot(up_ref[...], normed), 0.0).astype(BF16)
        out = stream + dot(down_ref[...], expanded)
        for i in range(half):
            out_ref[h * half + i] = out[:, i * lanes : (i + 1) * lanes].T.astype(BF16)


def temporal(me, weights, chunks, first, groups, total, so_far):
    width, lanes = chunks[0][0].shape[2:]
    count = len(chunks[0])
    sizes = [chunk[0].shape[1] for chunk in chunks]
    snaps = sum(sizes)

    def part(a):
        at = first if a.shape[0] == total else 0
        return pl.BlockSpec((1,) + a.shape[1:], lambda g, i: (g + at, 0, 0, 0))

    parts = [a for chunk in chunks for a in chunk]
    extra = [] if so_far is None else [so_far]
    return pl.pallas_call(
        functools.partial(temporal_kernel, sizes, count - 1),
        grid_spec=pltpu.PrefetchScalarGridSpec(
            num_scalar_prefetch=1,
            grid=(groups,),
            in_specs=[whole(a) for a in weights]
            + [part(a) for a in parts]
            + [pl.BlockSpec(memory_space=pl.ANY)] * len(extra),
            out_specs=pl.BlockSpec((snaps, lanes, width), lambda g, i: (0, g + first, 0)),
            scratch_shapes=[
                pltpu.VMEM((snaps * count, width, lanes), F32),
                pltpu.VMEM((snaps * count, width, lanes), F32),
                pltpu.VMEM((snaps, width, lanes), F32),
                pltpu.VMEM((snaps, width, lanes), F32),
                pltpu.VMEM((snaps, HEADS, lanes), F32),
                pltpu.VMEM((width, snaps * lanes), BF16),
            ],
        ),
        out_shape=jax.ShapeDtypeStruct((snaps, total * lanes, width), BF16),
        input_output_aliases={1 + len(weights) + len(parts): 0} if extra else {},
        compiler_params=pltpu.CompilerParams(vmem_limit_bytes=VMEM),
        cost_estimate=cost(10),
        name="temporal",
    )(me, *weights, *parts, *extra)


def send(a, k):
    return lax.ppermute(a, "vert", [(v, v ^ k) for v in range(lax.axis_size("vert"))])


def exchange_direct(blocks, want, inner):
    snaps = blocks.shape[0]
    count = lax.axis_size("vert")
    outer = count // inner
    wants = [send(want, k * inner) for k in range(1, outer)]
    layer = [blocks] + [send(blocks, j) for j in range(1, inner)]
    jobs = [
        (k - 1, [(j, k * inner + j) for j in range(inner)], 0, snaps) for k in range(1, outer)
    ]
    picked = pick(layer, [0] * inner, wants, jobs)
    arrived = [send(picked[k - 1], k * inner) for k in range(1, outer)]
    return [(0, snaps, [(a, 0) for a in layer + arrived])]


def exchange_forward(blocks, want):
    snaps = blocks.shape[0]
    layers = lambda pairs, x=0: [(a * 2 + i, b * 2 + (i ^ x)) for a, b in pairs for i in range(2)]
    go = lambda a, pairs, x=0: lax.ppermute(a, "vert", layers(pairs, x))
    cross = [(1, 2), (2, 1)]
    skip = [(0, 2), (3, 1)]
    ends = [(2, 3), (1, 0)]
    back = [(3, 2), (0, 1)]

    cut = snaps // 2
    first, rest = blocks[:cut], blocks[cut:]
    p1, p2, beside = go(first, cross), go(first, skip), send(first, 2)
    wants = [send(want, 1), go(want, back), go(want, back, 1)]
    rest, *wants = after((rest, *wants))

    def forward(own, beside, p1, p2, lo, cuts):
        srcs, hi = [own, beside, p1, p2], cuts[-1]
        jobs = [(0, [(0, 1), (1, 3)], lo, hi), (0, [(3, 5), (2, 7)], lo, hi)]
        spans = list(zip([lo] + cuts, cuts))
        for span in spans:
            jobs += [(1, [(2, 4), (3, 6)], *span), (2, [(2, 5), (3, 7)], *span)]
        x1, x2, *ends_of = pick(srcs, [lo] * 4, wants, jobs)
        sent = [(go(ends_of[2 * i], ends), go(ends_of[2 * i + 1], ends, 1)) for i in range(len(spans))]
        x1, x2 = send(x1, 1), go(x2, [(1, 1), (2, 2)], 1)
        return [
            (first, stop, [(a, lo) for a in (*srcs, x1, x2)] + [(a, first) for a in pair])
            for (first, stop), pair in zip(spans, sent)
        ]

    parts = forward(first, beside, p1, p2, 0, [cut])
    q1, q2, far = go(rest, cross), go(rest, skip), send(rest, 2)
    return parts + forward(rest, far, q1, q2, cut, [cut + (snaps - cut) // 2, snaps])


def gather_times(own):
    times = lax.axis_size("tm")
    got = [own] + [None] * (times - 1)
    for k in range(1, times):
        if k == 1 or k % 2 == 0:
            pairs = [(m, m ^ k) for m in range(times) if m < (m ^ k)]
            got[k] = lax.ppermute(own, "tm", pairs)
    return got


def pass_on(got, late):
    times = lax.axis_size("tm")
    got = list(got)
    for k in range(3, times, 2):
        pairs = [(m, m ^ 1) for m in range(times) if (m ^ (k - 1)) < m]
        got[k - 1], _ = after((got[k - 1], late))
        got[k] = lax.ppermute(got[k - 1], "tm", pairs)
    return got


def local(
    features,
    tile_cols,
    tile_vals,
    space_weight,
    positions,
    attn_proj,
    attn_out,
    norm_gain,
    mlp_up,
    mlp_down,
):
    snaps, verts, width = features.shape
    rows, tiles, size = tile_vals.shape[1:4]
    count = lax.axis_size("vert")
    outer, inner = split_axis(count)
    me_t = lax.axis_index("tm").astype(jnp.int32)
    me_v = lax.axis_index("vert").astype(jnp.int32)
    blocks = features.reshape(snaps, rows, size, width)

    forward = (outer, inner) == (4, 2)
    weights = (attn_proj, attn_out, norm_gain, mlp_up, mlp_down, space_weight)
    want, slots, pos, *weights, space_t = prepare(
        jnp.stack([me_v, me_t]), tile_cols, positions, weights, rows, count, inner, forward
    )
    me = me_t.reshape(1)
    parts = exchange_forward(blocks, want) if forward else exchange_direct(blocks, want, inner)

    started, owns = [], []
    for start, stop, srcs in parts:
        if owns:
            srcs[0] = (after((srcs[0][0], owns[-1]))[0], srcs[0][1])
        owns.append(spatial(slots, tile_vals, start, stop, space_t, pos, srcs, 1)[0])
        started.append(gather_times(owns[-1]))
    chunks = [pass_on(got, own) for got, own in zip(started, owns[1:] + owns[-1:])]
    return temporal(me, weights, chunks, 0, rows, rows, None)


def solution(mesh):
    placed = (
        P("tm", "vert", None),
        P("tm", "vert", None),
        P("tm", "vert", None, None, None),
        P(),
        P(),
        P(),
        P(),
        P(),
        P(),
        P(),
    )
    return jax.shard_map(
        local, mesh=mesh, in_specs=placed, out_specs=P("tm", "vert", None), check_vma=False
    )
```

```python
import functools
import math

import jax
import jax.numpy as jnp
from jax import lax
from jax.experimental import pallas as pl
from jax.experimental.pallas import tpu as pltpu
from jax.sharding import PartitionSpec as P

HEADS = 16
CAP = 4.0
EPS = 1e-05
VMEM = 24 * 1024 * 1024
BF16 = jnp.bfloat16
F32 = jnp.float32
after = lax.optimization_barrier


def split_axis(count):
    inner = 1
    while (inner * 2) * (inner * 2) <= count and count % (inner * 2) == 0:
        inner *= 2
    return count // inner, inner


def dot(a, b):
    return jnp.dot(a, b, preferred_element_type=F32)


def dot_nt(a, b):
    return lax.dot_general(a, b, (((1,), (1,)), ((), ())), preferred_element_type=F32)


def whole(a):
    return pl.BlockSpec(a.shape, lambda *i: (0,) * len(a.shape))


def near(a):
    return pltpu.with_memory_space_constraint(a, pltpu.VMEM)


def cost(us):
    return pl.CostEstimate(flops=int(us * 1.15e9), bytes_accessed=1024, transcendentals=0)


def lists_kernel(rows, count, inner, forward, at_ref, cols_ref, want_o, slot_o):
    me = at_ref[0]
    cols = cols_ref[...]
    rel = (cols // rows) ^ me
    loc = cols % rows
    slots = jnp.zeros_like(cols)
    for k in range(count):
        hit = rel == k
        least = lambda a: jnp.min(jnp.min(a, axis=2, keepdims=True), axis=1, keepdims=True)
        low = least(jnp.where(hit, loc, rows - 1))
        high = -least(jnp.where(hit, -loc, 0))
        want_o[:, :, 2 * k : 2 * k + 1] = low
        want_o[:, :, 2 * k + 1 : 2 * k + 2] = high
        second = jnp.where(loc == low, 0, 1)
        if forward:
            o = me // inner
            middle = (o == 1) | (o == 2)
            inside = {4: 3 * rows + loc, 5: 7 * rows + second, 6: 2 * rows + loc, 7: 6 * rows + second}
            if k < 4:
                at = {0: loc, 1: 4 * rows + second, 2: rows + loc, 3: 5 * rows + second}[k]
            else:
                at = jnp.where(middle, inside[k], (4 + k) * rows + second)
        elif k < inner:
            at = k * rows + loc
        else:
            at = inner * rows + (k - inner) * 2 + second
        slots = jnp.where(hit, at, slots)
    slot_o[...] = slots


def lists(at, cols, rows, count, inner, forward):
    outs = [
        jax.ShapeDtypeStruct((cols.shape[0], 1, 2 * count), jnp.int32),
        jax.ShapeDtypeStruct(cols.shape, jnp.int32),
    ]
    return pl.pallas_call(
        functools.partial(lists_kernel, rows, count, inner, forward),
        grid_spec=pltpu.PrefetchScalarGridSpec(
            num_scalar_prefetch=1,
            grid=(1,),
            in_specs=[whole(cols)],
            out_specs=[whole(a) for a in outs],
        ),
        out_shape=outs,
        cost_estimate=cost(1),
        name="lists",
    )(at, cols)


def weights_kernel(at_ref, pos_ref, qkv_ref, proj_ref, gain_ref, up_ref, down_ref, space_ref, *refs):
    pos_o, qkv_o, proj_o, gain_o, up_o, down_o, space_o, pos_s = refs
    width = proj_ref.shape[0]
    head_dim = width // HEADS
    snaps = pos_o.shape[0]
    pos_s[...] = pos_ref[...].astype(F32)
    pos_o[...] = pos_s[pl.ds(at_ref[1] * snaps, snaps), :]
    to = lax.broadcasted_iota(jnp.int32, (width, width), 0)
    source = lax.broadcasted_iota(jnp.int32, (width, width), 1)
    by_head = jnp.where((to % HEADS) * head_dim + to // HEADS == source, 1.0, 0.0).astype(BF16)
    for i in range(3):
        part = slice(i * width, (i + 1) * width)
        qkv_o[part, :] = dot_nt(by_head, qkv_ref[:, part]).astype(BF16)
    flip = lambda a: a.astype(F32).T.astype(BF16)
    proj_o[...] = dot_nt(flip(proj_ref[...]), by_head).astype(BF16)
    gain_o[...] = jnp.broadcast_to(gain_ref[...], gain_o.shape).T
    for i in range(up_ref.shape[1] // width):
        part = slice(i * width, (i + 1) * width)
        up_o[part, :] = flip(up_ref[:, part])
        down_o[:, part] = flip(down_ref[part, :])
    space_o[...] = flip(space_ref[...])


def turned(at, snaps, positions, qkv, proj, gain, up, down, space):
    width = proj.shape[0]
    ins = [positions, qkv, proj, gain.reshape(1, width), up, down, space]
    shape = jax.ShapeDtypeStruct
    outs = [
        shape((snaps, width), F32),
        shape((3 * width, width), BF16),
        shape((width, width), BF16),
        shape((width, width), F32),
        shape((up.shape[1], width), BF16),
        shape((width, down.shape[0]), BF16),
        shape((width, width), BF16),
    ]
    return pl.pallas_call(
        weights_kernel,
        grid_spec=pltpu.PrefetchScalarGridSpec(
            num_scalar_prefetch=1,
            grid=(1,),
            in_specs=[whole(a) for a in ins],
            out_specs=[whole(a) for a in outs],
            scratch_shapes=[pltpu.VMEM(positions.shape, F32)],
        ),
        out_shape=outs,
        compiler_params=pltpu.CompilerParams(vmem_limit_bytes=VMEM),
        cost_estimate=cost(2),
        name="turn_weights",
    )(at, *ins)


def pick_kernel(jobs, wants, offsets, *refs):
    outs = refs[len(refs) - len(jobs) :]
    want_refs, srcs = refs[:wants], refs[wants : len(refs) - len(jobs)]
    for (which, pairs, lo, _), out in zip(jobs, outs):
        for s in range(out.shape[0]):
            for j, (src, rel) in enumerate(pairs):
                for i in range(2):
                    block = want_refs[which][lo + s, 0, 2 * rel + i]
                    out[s, 2 * j + i] = srcs[src][lo + s - offsets[src], block]


def pick(srcs, offsets, wants, jobs):
    size, width = srcs[0].shape[2:]
    shapes = [
        jax.ShapeDtypeStruct((hi - lo, 2 * len(pairs), size, width), BF16)
        for _, pairs, lo, hi in jobs
    ]
    return pl.pallas_call(
        functools.partial(pick_kernel, jobs, len(wants), offsets),
        grid_spec=pltpu.PrefetchScalarGridSpec(
            num_scalar_prefetch=len(wants),
            grid=(1,),
            in_specs=[pl.BlockSpec(memory_space=pltpu.VMEM)] * len(srcs),
            out_specs=[whole(a) for a in shapes],
        ),
        out_shape=shapes,
        compiler_params=pltpu.CompilerParams(vmem_limit_bytes=VMEM),
        cost_estimate=cost(1),
        name="pick_blocks",
    )(*wants, *[near(a) for a in srcs])


def spatial_kernel(start, offsets, slot_ref, vals_ref, weight_ref, pos_ref, *refs):
    srcs, (*outs, held, vals, sums, own_sem, vals_sem) = refs[: len(offsets)], refs[len(offsets) :]
    snaps, rows, tiles, size, _ = vals.shape
    each = rows // len(outs)
    span = slice(start - offsets[0], start - offsets[0] + snaps)
    own = pltpu.make_async_copy(srcs[0].at[span], held.at[0], own_sem)
    own.start()
    arriving = []
    for s in range(snaps):
        arriving.append(pltpu.make_async_copy(vals_ref.at[start + s], vals.at[s], vals_sem.at[s]))
        arriving[s].start()
    unit = 1
    for src, offset in zip(srcs[1:], offsets[1:]):
        for first in range(0, src.shape[1], rows):
            n = min(rows, src.shape[1] - first)
            some = src[start - offset : start - offset + snaps, first : first + n]
            held[unit, :, :n] = some
            unit += 1
    own.wait()
    for s in range(snaps):
        arriving[s].wait()
        for r in range(rows):
            left = jnp.concatenate([vals[s, r, k] for k in range(tiles)], axis=1)
            right = []
            for k in range(tiles):
                slot = slot_ref[start + s, r, k]
                right.append(held[slot // rows, s, slot % rows])
            summed = dot(left, jnp.concatenate(right, axis=0)).astype(BF16)
            sums[(s * rows + r) * size : (s * rows + r + 1) * size, :] = summed
    for s in range(snaps):
        pos = pos_ref[start + s : start + s + 1, :]
        position = jnp.broadcast_to(pos, (size, pos.shape[1])).T
        some = sums[s * rows * size : (s + 1) * rows * size, :]
        hidden = jnp.maximum(dot_nt(weight_ref[...], some), 0.0).astype(BF16).astype(F32)
        for r in range(rows):
            mixed = hidden[:, r * size : (r + 1) * size] + position
            outs[r // each][r % each, s] = mixed.astype(BF16)


def spatial(slots, vals, start, stop, weight_t, pos, srcs, parts):
    rows, tiles, size, _ = vals.shape[1:]
    snaps = stop - start
    width = weight_t.shape[0]
    units = sum(-(-a.shape[1] // rows) for a, _ in srcs)
    anywhere = pl.BlockSpec(memory_space=pl.ANY)
    out = jax.ShapeDtypeStruct((rows // parts, snaps, width, size), BF16)
    return pl.pallas_call(
        functools.partial(spatial_kernel, start, [first for _, first in srcs]),
        grid_spec=pltpu.PrefetchScalarGridSpec(
            num_scalar_prefetch=1,
            grid=(1,),
            in_specs=[anywhere, whole(weight_t), whole(pos), anywhere]
            + [pl.BlockSpec(memory_space=pltpu.VMEM)] * (len(srcs) - 1),
            out_specs=[whole(out)] * parts,
            scratch_shapes=[
                pltpu.VMEM((units, snaps, rows, size, width), BF16),
                pltpu.VMEM((snaps, rows, tiles, size, size), BF16),
                pltpu.VMEM((snaps * rows * size, width), BF16),
                pltpu.SemaphoreType.DMA,
                pltpu.SemaphoreType.DMA((snaps,)),
            ],
        ),
        out_shape=[out] * parts,
        compiler_params=pltpu.CompilerParams(vmem_limit_bytes=VMEM),
        cost_estimate=cost(snaps),
        name="spatial",
    )(slots, vals, weight_t, pos, srcs[0][0], *[near(a) for a, _ in srcs[1:]])


def temporal_kernel(sizes, others, me_ref, qkv_ref, proj_ref, gain_ref, up_ref, down_ref, *refs):
    count = 1 + others
    arrays = refs[: count * len(sizes)]
    out_ref, k_s, v_s, q_s, acc_s, total_s, att_s = refs[-7:]
    snaps = sum(sizes)
    width, lanes = arrays[0].shape[2:]
    head_dim = width // HEADS
    me, g = me_ref[0], pl.program_id(0)
    scale = 1.0 / (CAP * math.sqrt(head_dim))
    steep = CAP * math.log2(math.e)

    def held(i):
        return [arrays[c * count + i][g, s] for c, n in enumerate(sizes) for s in range(n)]

    def project(i):
        skip = 0 if i == 0 else width
        base = (me ^ i) * snaps
        found = held(i)
        for first in range(0, snaps, 4):
            some = found[first : first + 4]
            got = dot(qkv_ref[skip:, :], jnp.concatenate(some, axis=1)).astype(BF16).astype(F32)
            for j in range(len(some)):
                part = got[:, j * lanes : (j + 1) * lanes]
                if i == 0:
                    q_s[first + j] = part[:width] * scale
                k_s[base + first + j] = part[width - skip : 2 * width - skip]
                v_s[base + first + j] = part[2 * width - skip :]

    project(0)
    for i in range(1, count):
        pl.when((me ^ i) < me)(functools.partial(project, i))

    def attend(at, keys, fresh=False):
        q = [q_s[at, d * HEADS : (d + 1) * HEADS] for d in range(head_dim)]
        total, acc = None, None
        for u in keys:
            row = lambda ref, d: ref[u, d * HEADS : (d + 1) * HEADS]
            raw = q[0] * row(k_s, 0)
            for d in range(1, head_dim):
                raw = raw + q[d] * row(k_s, d)
            e = jnp.exp2(steep * jnp.tanh(raw))
            if total is None:
                total, acc = e, [e * row(v_s, d) for d in range(head_dim)]
            else:
                total = total + e
                acc = [acc[d] + e * row(v_s, d) for d in range(head_dim)]
        for d in range(head_dim):
            span = slice(d * HEADS, (d + 1) * HEADS)
            acc_s[at, span] = acc[d] if fresh else acc_s[at, span] + acc[d]
        total_s[at] = total if fresh else total_s[at] + total

    for s in range(snaps):
        attend(s, [me * snaps + j for j in range(s + 1)], fresh=True)

    def earlier(m, none):
        for at in range(snaps):
            attend(at, [m * snaps + j for j in range(snaps)])
        return none

    lax.fori_loop(0, me, earlier, 0)

    mine = held(0)
    for at in range(snaps):
        inv = 1.0 / total_s[at]
        for d in range(head_dim):
            span = slice(d * HEADS, (d + 1) * HEADS)
            att_s[span, at * lanes : (at + 1) * lanes] = (acc_s[at, span] * inv).astype(BF16)
    half = snaps // 2
    for h in range(2):
        span = slice(h * half * lanes, (h + 1) * half * lanes)
        base = jnp.concatenate(mine[h * half : (h + 1) * half], axis=1).astype(F32)
        stream = base + dot(proj_ref[...], att_s[:, span])
        centre = jnp.mean(stream, axis=0, keepdims=True)
        away = stream - centre
        spread = jnp.mean(away * away, axis=0, keepdims=True)
        gain = jnp.concatenate([gain_ref[...]] * half, axis=1)
        normed = (away * lax.rsqrt(spread + EPS) * gain).astype(BF16)
        expanded = jnp.maximum(dot(up_ref[...], normed), 0.0).astype(BF16)
        out = stream + dot(down_ref[...], expanded)
        for i in range(half):
            out_ref[h * half + i] = out[:, i * lanes : (i + 1) * lanes].T.astype(BF16)


def temporal(me, weights, chunks):
    groups, _, width, lanes = chunks[0][0].shape
    count = len(chunks[0])
    sizes = [chunk[0].shape[1] for chunk in chunks]
    snaps = sum(sizes)

    parts = [a for chunk in chunks for a in chunk]
    return pl.pallas_call(
        functools.partial(temporal_kernel, sizes, count - 1),
        grid_spec=pltpu.PrefetchScalarGridSpec(
            num_scalar_prefetch=1,
            grid=(groups,),
            in_specs=[whole(a) for a in weights]
            + [pl.BlockSpec(memory_space=pltpu.VMEM)] * len(parts),
            out_specs=pl.BlockSpec((snaps, lanes, width), lambda g, i: (0, g, 0)),
            scratch_shapes=[
                pltpu.VMEM((snaps * count, width, lanes), F32),
                pltpu.VMEM((snaps * count, width, lanes), F32),
                pltpu.VMEM((snaps, width, lanes), F32),
                pltpu.VMEM((snaps, width, lanes), F32),
                pltpu.VMEM((snaps, HEADS, lanes), F32),
                pltpu.VMEM((width, snaps * lanes), BF16),
            ],
        ),
        out_shape=jax.ShapeDtypeStruct((snaps, groups * lanes, width), BF16),
        compiler_params=pltpu.CompilerParams(vmem_limit_bytes=VMEM),
        cost_estimate=cost(10),
        name="temporal",
    )(me, *weights, *[near(a) for a in parts])


def send(a, k):
    return lax.ppermute(a, "vert", [(v, v ^ k) for v in range(lax.axis_size("vert"))])


def exchange_direct(blocks, want, inner):
    snaps = blocks.shape[0]
    count = lax.axis_size("vert")
    outer = count // inner
    wants = [send(want, k * inner) for k in range(1, outer)]
    layer = [blocks] + [send(blocks, j) for j in range(1, inner)]
    jobs = [
        (k - 1, [(j, k * inner + j) for j in range(inner)], 0, snaps) for k in range(1, outer)
    ]
    picked = pick(layer, [0] * inner, wants, jobs)
    arrived = [send(picked[k - 1], k * inner) for k in range(1, outer)]
    return [(0, snaps, lambda before: [(a, 0) for a in layer + arrived])]


def exchange_forward(blocks, want):
    snaps = blocks.shape[0]
    layers = lambda pairs, x=0: [(a * 2 + i, b * 2 + (i ^ x)) for a, b in pairs for i in range(2)]
    go = lambda a, pairs, x=0: lax.ppermute(a, "vert", layers(pairs, x))
    cross = [(1, 2), (2, 1)]
    ends = [(2, 3), (1, 0)]
    back = [(3, 2), (0, 1)]
    inside = [(1, 1), (2, 2)]

    p1, beside = go(blocks, cross), send(blocks, 2)
    wants = [send(want, 1), None, None]
    (xo,) = pick([blocks], [0], wants[:1], [(0, [(0, 1)], 0, snaps)])
    xo = send(xo, 1)
    both = go(jnp.concatenate([want, wants[0]], axis=1), back)
    beside, both, xo, p1 = after((beside, both, xo, p1))
    wants[1:] = both[:, :1], both[:, 1:]

    p2 = go(beside, cross)
    jobs = [(1, [(0, 4)], 0, snaps), (2, [(0, 5)], 0, snaps), (0, [(0, 7)], 0, snaps)]
    f0, f1, x1, xn = pick([p1, beside], [0, 0], wants, jobs + [(0, [(1, 3)], 0, snaps)])
    f0, f1, x1, xn = go(f0, ends), go(f1, ends, 1), go(x1, inside, 1), send(xn, 1)

    cuts = sorted({0, snaps // 4, -(-5 * snaps // 8), snaps})
    spans = list(zip(cuts, cuts[1:]))
    jobs = [(0, [(0, 5)], 0, snaps)]
    for span in spans:
        jobs += [(1, [(0, 6)], *span), (2, [(0, 7)], *span)]
    x2, *late = pick([p2], [0], wants, jobs)
    x2 = go(x2, inside, 1)
    all_snaps = [(a, 0) for a in (blocks, beside, p1, p2, xo, xn, x1, x2, f0, f1)]

    def part(span, a, b):
        def get(before):
            pair = (a, b) if before is None else after((a, b, before))[:2]
            sent = go(pair[0], ends), go(pair[1], ends, 1)
            return all_snaps + [(c, span[0]) for c in sent]

        return (*span, get)

    return [part(span, a, b) for span, a, b in zip(spans, late[::2], late[1::2])]


def gather_times(own):
    times = lax.axis_size("tm")
    got = [own] + [None] * (times - 1)
    for k in range(1, times):
        if k == 1 or k % 2 == 0:
            pairs = [(m, m ^ k) for m in range(times) if m < (m ^ k)]
            got[k] = lax.ppermute(own, "tm", pairs)
    return got


def pass_on(got, late):
    times = lax.axis_size("tm")
    got = list(got)
    for k in range(3, times, 2):
        pairs = [(m, m ^ 1) for m in range(times) if (m ^ (k - 1)) < m]
        got[k - 1], _ = after((got[k - 1], late))
        got[k] = lax.ppermute(got[k - 1], "tm", pairs)
    return got


def local(
    features,
    tile_cols,
    tile_vals,
    space_weight,
    positions,
    attn_proj,
    attn_out,
    norm_gain,
    mlp_up,
    mlp_down,
):
    snaps, verts, width = features.shape
    rows, tiles, size = tile_vals.shape[1:4]
    count = lax.axis_size("vert")
    outer, inner = split_axis(count)
    me_t = lax.axis_index("tm").astype(jnp.int32)
    me_v = lax.axis_index("vert").astype(jnp.int32)
    blocks = features.reshape(snaps, rows, size, width)

    forward = (outer, inner) == (4, 2)
    at = jnp.stack([me_v, me_t])
    want, slots = lists(at, tile_cols, rows, count, inner, forward)
    pos, *weights, space_t = turned(
        at, snaps, positions, attn_proj, attn_out, norm_gain, mlp_up, mlp_down, space_weight
    )
    me = me_t.reshape(1)
    parts = exchange_forward(blocks, want) if forward else exchange_direct(blocks, want, inner)

    started, owns = [], []
    held = [get(None) for _, _, get in parts[:2]]
    for c, (start, stop, get) in enumerate(parts):
        srcs = held[c] if c < 2 else get(owns[c - 2])
        if owns:
            sent = [a for a in started[c - 2] if a is not None] if c > 1 else []
            srcs = [(after((srcs[0][0], owns[-1], *sent))[0], srcs[0][1])] + srcs[1:]
        owns.append(spatial(slots, tile_vals, start, stop, space_t, pos, srcs, 1)[0])
        started.append(gather_times(owns[-1]))
    chunks = [pass_on(got, own) for got, own in zip(started, owns[1:] + owns[-1:])]
    return temporal(me, weights, chunks)


def solution(mesh):
    placed = (
        P("tm", "vert", None),
        P("tm", "vert", None),
        P("tm", "vert", None, None, None),
        P(),
        P(),
        P(),
        P(),
        P(),
        P(),
        P(),
    )
    return jax.shard_map(
        local, mesh=mesh, in_specs=placed, out_specs=P("tm", "vert", None), check_vma=False
    )
```

```python
import functools
import math

import jax
import jax.numpy as jnp
from jax import lax
from jax.experimental import pallas as pl
from jax.experimental.pallas import tpu as pltpu
from jax.sharding import PartitionSpec as P

HEADS = 16
CAP = 4.0
EPS = 1e-05
VMEM = 24 * 1024 * 1024
BF16 = jnp.bfloat16
F32 = jnp.float32
after = lax.optimization_barrier


def split_axis(count):
    inner = 1
    while (inner * 2) * (inner * 2) <= count and count % (inner * 2) == 0:
        inner *= 2
    return count // inner, inner


def dot(a, b):
    return jnp.dot(a, b, preferred_element_type=F32)


def dot_nt(a, b):
    return lax.dot_general(a, b, (((1,), (1,)), ((), ())), preferred_element_type=F32)


def whole(a):
    return pl.BlockSpec(a.shape, lambda *i: (0,) * len(a.shape))


def near(a):
    return pltpu.with_memory_space_constraint(a, pltpu.VMEM)


def cost(us):
    return pl.CostEstimate(flops=int(us * 1.15e9), bytes_accessed=1024, transcendentals=0)


def lists_kernel(rows, count, inner, forward, at_ref, cols_ref, want_o, slot_o):
    me = at_ref[0]
    cols = cols_ref[...]
    rel = (cols // rows) ^ me
    loc = cols % rows
    slots = jnp.zeros_like(cols)
    for k in range(count):
        hit = rel == k
        least = lambda a: jnp.min(jnp.min(a, axis=2, keepdims=True), axis=1, keepdims=True)
        low = least(jnp.where(hit, loc, rows - 1))
        high = -least(jnp.where(hit, -loc, 0))
        want_o[:, :, 2 * k : 2 * k + 1] = low
        want_o[:, :, 2 * k + 1 : 2 * k + 2] = high
        second = jnp.where(loc == low, 0, 1)
        if forward:
            o = me // inner
            middle = (o == 1) | (o == 2)
            inside = {4: 3 * rows + loc, 5: 7 * rows + second, 6: 2 * rows + loc, 7: 6 * rows + second}
            if k < 4:
                at = {0: loc, 1: 4 * rows + second, 2: rows + loc, 3: 5 * rows + second}[k]
            else:
                at = jnp.where(middle, inside[k], (4 + k) * rows + second)
        elif k < inner:
            at = k * rows + loc
        else:
            at = inner * rows + (k - inner) * 2 + second
        slots = jnp.where(hit, at, slots)
    slot_o[...] = slots


def lists(at, cols, rows, count, inner, forward):
    outs = [
        jax.ShapeDtypeStruct((cols.shape[0], 1, 2 * count), jnp.int32),
        jax.ShapeDtypeStruct(cols.shape, jnp.int32),
    ]
    return pl.pallas_call(
        functools.partial(lists_kernel, rows, count, inner, forward),
        grid_spec=pltpu.PrefetchScalarGridSpec(
            num_scalar_prefetch=1,
            grid=(1,),
            in_specs=[whole(cols)],
            out_specs=[whole(a) for a in outs],
        ),
        out_shape=outs,
        cost_estimate=cost(1),
        name="lists",
    )(at, cols)


def weights_kernel(at_ref, pos_ref, qkv_ref, proj_ref, gain_ref, up_ref, down_ref, space_ref, *refs):
    pos_o, qkv_o, proj_o, gain_o, up_o, down_o, space_o, pos_s = refs
    width = proj_ref.shape[0]
    head_dim = width // HEADS
    snaps = pos_o.shape[0]
    pos_s[...] = pos_ref[...].astype(F32)
    pos_o[...] = pos_s[pl.ds(at_ref[1] * snaps, snaps), :]
    to = lax.broadcasted_iota(jnp.int32, (width, width), 0)
    source = lax.broadcasted_iota(jnp.int32, (width, width), 1)
    by_head = jnp.where((to % HEADS) * head_dim + to // HEADS == source, 1.0, 0.0).astype(BF16)
    for i in range(3):
        part = slice(i * width, (i + 1) * width)
        qkv_o[part, :] = dot_nt(by_head, qkv_ref[:, part]).astype(BF16)
    flip = lambda a: a.astype(F32).T.astype(BF16)
    proj_o[...] = dot_nt(flip(proj_ref[...]), by_head).astype(BF16)
    gain_o[...] = jnp.broadcast_to(gain_ref[...], gain_o.shape).T
    for i in range(up_ref.shape[1] // width):
        part = slice(i * width, (i + 1) * width)
        up_o[part, :] = flip(up_ref[:, part])
        down_o[:, part] = flip(down_ref[part, :])
    space_o[...] = flip(space_ref[...])


def turned(at, snaps, positions, qkv, proj, gain, up, down, space):
    width = proj.shape[0]
    ins = [positions, qkv, proj, gain.reshape(1, width), up, down, space]
    shape = jax.ShapeDtypeStruct
    outs = [
        shape((snaps, width), F32),
        shape((3 * width, width), BF16),
        shape((width, width), BF16),
        shape((width, width), F32),
        shape((up.shape[1], width), BF16),
        shape((width, down.shape[0]), BF16),
        shape((width, width), BF16),
    ]
    return pl.pallas_call(
        weights_kernel,
        grid_spec=pltpu.PrefetchScalarGridSpec(
            num_scalar_prefetch=1,
            grid=(1,),
            in_specs=[whole(a) for a in ins],
            out_specs=[whole(a) for a in outs],
            scratch_shapes=[pltpu.VMEM(positions.shape, F32)],
        ),
        out_shape=outs,
        compiler_params=pltpu.CompilerParams(vmem_limit_bytes=VMEM),
        cost_estimate=cost(2),
        name="turn_weights",
    )(at, *ins)


def pick_kernel(jobs, wants, offsets, *refs):
    outs = refs[len(refs) - len(jobs) :]
    want_refs, srcs = refs[:wants], refs[wants : len(refs) - len(jobs)]
    for (which, pairs, lo, _), out in zip(jobs, outs):
        for s in range(out.shape[0]):
            for j, (src, rel) in enumerate(pairs):
                for i in range(2):
                    block = want_refs[which][lo + s, 0, 2 * rel + i]
                    out[s, 2 * j + i] = srcs[src][lo + s - offsets[src], block]


def pick(srcs, offsets, wants, jobs):
    size, width = srcs[0].shape[2:]
    shapes = [
        jax.ShapeDtypeStruct((hi - lo, 2 * len(pairs), size, width), BF16)
        for _, pairs, lo, hi in jobs
    ]
    return pl.pallas_call(
        functools.partial(pick_kernel, jobs, len(wants), offsets),
        grid_spec=pltpu.PrefetchScalarGridSpec(
            num_scalar_prefetch=len(wants),
            grid=(1,),
            in_specs=[pl.BlockSpec(memory_space=pltpu.VMEM)] * len(srcs),
            out_specs=[whole(a) for a in shapes],
        ),
        out_shape=shapes,
        compiler_params=pltpu.CompilerParams(vmem_limit_bytes=VMEM),
        cost_estimate=cost(1),
        name="pick_blocks",
    )(*wants, *[near(a) for a in srcs])


def spatial_kernel(start, offsets, slot_ref, vals_ref, weight_ref, pos_ref, *refs):
    srcs, (*outs, held, vals, sums, own_sem, vals_sem) = refs[: len(offsets)], refs[len(offsets) :]
    snaps, rows, tiles, size, _ = vals.shape
    each = rows // len(outs)
    span = slice(start - offsets[0], start - offsets[0] + snaps)
    own = pltpu.make_async_copy(srcs[0].at[span], held.at[0], own_sem)
    own.start()
    arriving = []
    for s in range(snaps):
        arriving.append(pltpu.make_async_copy(vals_ref.at[start + s], vals.at[s], vals_sem.at[s]))
        arriving[s].start()
    unit = 1
    for src, offset in zip(srcs[1:], offsets[1:]):
        for first in range(0, src.shape[1], rows):
            n = min(rows, src.shape[1] - first)
            some = src[start - offset : start - offset + snaps, first : first + n]
            held[unit, :, :n] = some
            unit += 1
    own.wait()
    for s in range(snaps):
        arriving[s].wait()
        for r in range(rows):
            left = jnp.concatenate([vals[s, r, k] for k in range(tiles)], axis=1)
            right = []
            for k in range(tiles):
                slot = slot_ref[start + s, r, k]
                right.append(held[slot // rows, s, slot % rows])
            summed = dot(left, jnp.concatenate(right, axis=0)).astype(BF16)
            sums[(s * rows + r) * size : (s * rows + r + 1) * size, :] = summed
    for s in range(snaps):
        pos = pos_ref[start + s : start + s + 1, :]
        position = jnp.broadcast_to(pos, (size, pos.shape[1])).T
        some = sums[s * rows * size : (s + 1) * rows * size, :]
        hidden = jnp.maximum(dot_nt(weight_ref[...], some), 0.0).astype(BF16).astype(F32)
        for r in range(rows):
            mixed = hidden[:, r * size : (r + 1) * size] + position
            outs[r // each][r % each, s] = mixed.astype(BF16)


def spatial(slots, vals, start, stop, weight_t, pos, srcs, parts):
    rows, tiles, size, _ = vals.shape[1:]
    snaps = stop - start
    width = weight_t.shape[0]
    units = sum(-(-a.shape[1] // rows) for a, _ in srcs)
    anywhere = pl.BlockSpec(memory_space=pl.ANY)
    out = jax.ShapeDtypeStruct((rows // parts, snaps, width, size), BF16)
    return pl.pallas_call(
        functools.partial(spatial_kernel, start, [first for _, first in srcs]),
        grid_spec=pltpu.PrefetchScalarGridSpec(
            num_scalar_prefetch=1,
            grid=(1,),
            in_specs=[anywhere, whole(weight_t), whole(pos), anywhere]
            + [pl.BlockSpec(memory_space=pltpu.VMEM)] * (len(srcs) - 1),
            out_specs=[whole(out)] * parts,
            scratch_shapes=[
                pltpu.VMEM((units, snaps, rows, size, width), BF16),
                pltpu.VMEM((snaps, rows, tiles, size, size), BF16),
                pltpu.VMEM((snaps * rows * size, width), BF16),
                pltpu.SemaphoreType.DMA,
                pltpu.SemaphoreType.DMA((snaps,)),
            ],
        ),
        out_shape=[out] * parts,
        compiler_params=pltpu.CompilerParams(vmem_limit_bytes=VMEM),
        cost_estimate=cost(snaps),
        name="spatial",
    )(slots, vals, weight_t, pos, srcs[0][0], *[near(a) for a, _ in srcs[1:]])


def scales(width):
    return 1.0 / (CAP * math.sqrt(width // HEADS)), CAP * math.log2(math.e)


def attend(q_ref, k_ref, v_ref, at, keys, sums):
    width = q_ref.shape[1]
    spans = [slice(d, d + HEADS) for d in range(0, width, HEADS)]
    steep = scales(width)[1]
    q = [q_ref[at, span] for span in spans]
    total, acc = sums if sums else (None, None)
    for u in keys:
        raw = q[0] * k_ref[u, spans[0]]
        for d in range(1, len(spans)):
            raw = raw + q[d] * k_ref[u, spans[d]]
        e = jnp.exp2(steep * jnp.tanh(raw))
        values = [e * v_ref[u, span] for span in spans]
        total = e if total is None else total + e
        acc = values if acc is None else [one + more for one, more in zip(acc, values)]
    return total, acc


def own_kernel(sizes, qkv_ref, *refs):
    arrays = refs[: len(sizes)]
    q_out, acc_out, total_out, q_s, k_s, v_s = refs[len(sizes) :]
    snaps = sum(sizes)
    g = pl.program_id(0)
    width, lanes = arrays[0].shape[2:]
    scale = scales(width)[0]
    found = [a[g, s] for a, n in zip(arrays, sizes) for s in range(n)]
    for first in range(0, snaps, 4):
        some = found[first : first + 4]
        got = dot(qkv_ref[...], jnp.concatenate(some, axis=1)).astype(BF16)
        for j in range(len(some)):
            part = got[:, j * lanes : (j + 1) * lanes]
            q_out[0, first + j] = part[:width]
            q_s[first + j] = part[:width].astype(F32) * scale
            k_s[first + j] = part[width : 2 * width].astype(F32)
            v_s[first + j] = part[2 * width :].astype(F32)
    for s in range(snaps):
        total, acc = attend(q_s, k_s, v_s, s, range(s + 1), None)
        total_out[0, s] = total
        for d, one in enumerate(acc):
            acc_out[0, s, d * HEADS : (d + 1) * HEADS] = one


def own_part(qkv_t, arrays):
    groups, _, width, lanes = arrays[0].shape
    sizes = [a.shape[1] for a in arrays]
    snaps = sum(sizes)
    shape = jax.ShapeDtypeStruct
    outs = [
        shape((groups, snaps, width, lanes), BF16),
        shape((groups, snaps, width, lanes), F32),
        shape((groups, snaps, HEADS, lanes), F32),
    ]
    return pl.pallas_call(
        functools.partial(own_kernel, sizes),
        grid=(groups,),
        in_specs=[whole(qkv_t)] + [pl.BlockSpec(memory_space=pltpu.VMEM)] * len(arrays),
        out_specs=[pl.BlockSpec((1,) + a.shape[1:], lambda g: (g, 0, 0, 0)) for a in outs],
        scratch_shapes=[pltpu.VMEM((snaps, width, lanes), F32)] * 3,
        out_shape=outs,
        compiler_params=pltpu.CompilerParams(vmem_limit_bytes=VMEM),
        cost_estimate=cost(6),
        name="temporal_own",
    )(qkv_t, *[near(a) for a in arrays])


def temporal_kernel(sizes, others, me_ref, qkv_ref, proj_ref, gain_ref, up_ref, down_ref, *refs):
    count = 1 + others
    arrays = refs[: count * len(sizes)]
    q_ref, acc_ref, total_ref, out_ref, k_s, v_s, q_s, acc_s, total_s, att_s = refs[-10:]
    snaps = sum(sizes)
    width, lanes = arrays[0].shape[2:]
    me, g = me_ref[0], pl.program_id(0)
    scale = scales(width)[0]
    spans = [slice(d, d + HEADS) for d in range(0, width, HEADS)]

    def held(i):
        return [arrays[c * count + i][g, s] for c, n in enumerate(sizes) for s in range(n)]

    def project(i):
        base = (me ^ i) * snaps
        found = held(i)
        for first in range(0, snaps, 4):
            some = found[first : first + 4]
            got = dot(qkv_ref[width:, :], jnp.concatenate(some, axis=1)).astype(BF16).astype(F32)
            for j in range(len(some)):
                part = got[:, j * lanes : (j + 1) * lanes]
                k_s[base + first + j] = part[:width]
                v_s[base + first + j] = part[width:]

    for i in range(1, count):
        pl.when((me ^ i) < me)(functools.partial(project, i))
    for at in range(snaps):
        q_s[at] = q_ref[g, at].astype(F32) * scale
        acc_s[at] = acc_ref[g, at]
        total_s[at] = total_ref[g, at]

    def earlier(m, none):
        keys = [m * snaps + j for j in range(snaps)]
        for at in range(snaps):
            sums = total_s[at], [acc_s[at, span] for span in spans]
            total_s[at], acc = attend(q_s, k_s, v_s, at, keys, sums)
            for span, one in zip(spans, acc):
                acc_s[at, span] = one
        return none

    lax.fori_loop(0, me, earlier, 0)

    mine = held(0)
    for at in range(snaps):
        inv = 1.0 / total_s[at]
        for span in spans:
            att_s[span, at * lanes : (at + 1) * lanes] = (acc_s[at, span] * inv).astype(BF16)
    half = snaps // 2
    for h in range(2):
        span = slice(h * half * lanes, (h + 1) * half * lanes)
        base = jnp.concatenate(mine[h * half : (h + 1) * half], axis=1).astype(F32)
        stream = base + dot(proj_ref[...], att_s[:, span])
        centre = jnp.mean(stream, axis=0, keepdims=True)
        away = stream - centre
        spread = jnp.mean(away * away, axis=0, keepdims=True)
        gain = jnp.concatenate([gain_ref[...]] * half, axis=1)
        normed = (away * lax.rsqrt(spread + EPS) * gain).astype(BF16)
        expanded = jnp.maximum(dot(up_ref[...], normed), 0.0).astype(BF16)
        out = stream + dot(down_ref[...], expanded)
        for i in range(half):
            out_ref[h * half + i] = out[:, i * lanes : (i + 1) * lanes].T.astype(BF16)


def temporal(me, weights, chunks, own):
    groups, _, width, lanes = chunks[0][0].shape
    count = len(chunks[0])
    sizes = [chunk[0].shape[1] for chunk in chunks]
    snaps = sum(sizes)
    parts = [a for chunk in chunks for a in chunk] + list(own)
    return pl.pallas_call(
        functools.partial(temporal_kernel, sizes, count - 1),
        grid_spec=pltpu.PrefetchScalarGridSpec(
            num_scalar_prefetch=1,
            grid=(groups,),
            in_specs=[whole(a) for a in weights]
            + [pl.BlockSpec(memory_space=pltpu.VMEM)] * len(parts),
            out_specs=pl.BlockSpec((snaps, lanes, width), lambda g, i: (0, g, 0)),
            scratch_shapes=[
                pltpu.VMEM((snaps * count, width, lanes), F32),
                pltpu.VMEM((snaps * count, width, lanes), F32),
                pltpu.VMEM((snaps, width, lanes), F32),
                pltpu.VMEM((snaps, width, lanes), F32),
                pltpu.VMEM((snaps, HEADS, lanes), F32),
                pltpu.VMEM((width, snaps * lanes), BF16),
            ],
        ),
        out_shape=jax.ShapeDtypeStruct((snaps, groups * lanes, width), BF16),
        compiler_params=pltpu.CompilerParams(vmem_limit_bytes=VMEM),
        cost_estimate=cost(10),
        name="temporal",
    )(me, *weights, *[near(a) for a in parts])


def send(a, k):
    return lax.ppermute(a, "vert", [(v, v ^ k) for v in range(lax.axis_size("vert"))])


def exchange_direct(blocks, want, inner):
    snaps = blocks.shape[0]
    count = lax.axis_size("vert")
    outer = count // inner
    wants = [send(want, k * inner) for k in range(1, outer)]
    layer = [blocks] + [send(blocks, j) for j in range(1, inner)]
    jobs = [
        (k - 1, [(j, k * inner + j) for j in range(inner)], 0, snaps) for k in range(1, outer)
    ]
    picked = pick(layer, [0] * inner, wants, jobs)
    arrived = [send(picked[k - 1], k * inner) for k in range(1, outer)]
    return [(0, snaps, lambda before: [(a, 0) for a in layer + arrived])]


def exchange_forward(blocks, want):
    snaps = blocks.shape[0]
    layers = lambda pairs, x=0: [(a * 2 + i, b * 2 + (i ^ x)) for a, b in pairs for i in range(2)]
    go = lambda a, pairs, x=0: lax.ppermute(a, "vert", layers(pairs, x))
    cross = [(1, 2), (2, 1)]
    ends = [(2, 3), (1, 0)]
    back = [(3, 2), (0, 1)]
    inside = [(1, 1), (2, 2)]

    p1, beside = go(blocks, cross), send(blocks, 2)
    wants = [send(want, 1), None, None]
    (xo,) = pick([blocks], [0], wants[:1], [(0, [(0, 1)], 0, snaps)])
    xo = send(xo, 1)
    both = go(jnp.concatenate([want, wants[0]], axis=1), back)
    beside, both, xo, p1 = after((beside, both, xo, p1))
    wants[1:] = both[:, :1], both[:, 1:]

    p2 = go(beside, cross)
    jobs = [(1, [(0, 4)], 0, snaps), (2, [(0, 5)], 0, snaps), (0, [(0, 7)], 0, snaps)]
    f0, f1, x1, xn = pick([p1, beside], [0, 0], wants, jobs + [(0, [(1, 3)], 0, snaps)])
    f0, f1, x1, xn = go(f0, ends), go(f1, ends, 1), go(x1, inside, 1), send(xn, 1)

    cuts = sorted({0, snaps // 4, -(-5 * snaps // 8), snaps})
    spans = list(zip(cuts, cuts[1:]))
    jobs = [(0, [(0, 5)], 0, snaps)]
    for span in spans:
        jobs += [(1, [(0, 6)], *span), (2, [(0, 7)], *span)]
    x2, *late = pick([p2], [0], wants, jobs)
    x2 = go(x2, inside, 1)
    all_snaps = [(a, 0) for a in (blocks, beside, p1, p2, xo, xn, x1, x2, f0, f1)]

    def part(span, a, b):
        def get(before):
            pair = (a, b) if before is None else after((a, b, before))[:2]
            sent = go(pair[0], ends), go(pair[1], ends, 1)
            return all_snaps + [(c, span[0]) for c in sent]

        return (*span, get)

    return [part(span, a, b) for span, a, b in zip(spans, late[::2], late[1::2])]


def gather_times(own):
    times = lax.axis_size("tm")
    got = [own] + [None] * (times - 1)
    for k in range(1, times):
        if k == 1 or k % 2 == 0:
            pairs = [(m, m ^ k) for m in range(times) if m < (m ^ k)]
            got[k] = lax.ppermute(own, "tm", pairs)
    return got


def pass_on(got, late):
    times = lax.axis_size("tm")
    got = list(got)
    for k in range(3, times, 2):
        pairs = [(m, m ^ 1) for m in range(times) if (m ^ (k - 1)) < m]
        got[k - 1], _ = after((got[k - 1], late))
        got[k] = lax.ppermute(got[k - 1], "tm", pairs)
    return got


def local(
    features,
    tile_cols,
    tile_vals,
    space_weight,
    positions,
    attn_proj,
    attn_out,
    norm_gain,
    mlp_up,
    mlp_down,
):
    snaps, verts, width = features.shape
    rows, tiles, size = tile_vals.shape[1:4]
    count = lax.axis_size("vert")
    outer, inner = split_axis(count)
    me_t = lax.axis_index("tm").astype(jnp.int32)
    me_v = lax.axis_index("vert").astype(jnp.int32)
    blocks = features.reshape(snaps, rows, size, width)

    forward = (outer, inner) == (4, 2)
    at = jnp.stack([me_v, me_t])
    want, slots = lists(at, tile_cols, rows, count, inner, forward)
    pos, *weights, space_t = turned(
        at, snaps, positions, attn_proj, attn_out, norm_gain, mlp_up, mlp_down, space_weight
    )
    me = me_t.reshape(1)
    parts = exchange_forward(blocks, want) if forward else exchange_direct(blocks, want, inner)

    started, owns = [], []
    held = [get(None) for _, _, get in parts[:2]]
    for c, (start, stop, get) in enumerate(parts):
        srcs = held[c] if c < 2 else get(owns[c - 2])
        if owns:
            sent = [a for a in started[c - 2] if a is not None] if c > 1 else []
            srcs = [(after((srcs[0][0], owns[-1], *sent))[0], srcs[0][1])] + srcs[1:]
        owns.append(spatial(slots, tile_vals, start, stop, space_t, pos, srcs, 1)[0])
        started.append(gather_times(owns[-1]))
    chunks = [pass_on(got, own) for got, own in zip(started, owns[1:] + owns[-1:])]
    return temporal(me, weights, chunks, own_part(weights[0], owns))


def solution(mesh):
    placed = (
        P("tm", "vert", None),
        P("tm", "vert", None),
        P("tm", "vert", None, None, None),
        P(),
        P(),
        P(),
        P(),
        P(),
        P(),
        P(),
    )
    return jax.shard_map(
        local, mesh=mesh, in_specs=placed, out_specs=P("tm", "vert", None), check_vma=False
    )
```

```python
import functools
import math

import jax
import jax.numpy as jnp
from jax import lax
from jax.experimental import pallas as pl
from jax.experimental.pallas import tpu as pltpu
from jax.sharding import PartitionSpec as P

HEADS = 16
CAP = 4.0
EPS = 1e-05
VMEM = 24 * 1024 * 1024
BF16 = jnp.bfloat16
F32 = jnp.float32
after = lax.optimization_barrier


def split_axis(count):
    inner = 1
    while (inner * 2) * (inner * 2) <= count and count % (inner * 2) == 0:
        inner *= 2
    return count // inner, inner


def dot(a, b):
    return jnp.dot(a, b, preferred_element_type=F32)


def dot_nt(a, b):
    return lax.dot_general(a, b, (((1,), (1,)), ((), ())), preferred_element_type=F32)


def whole(a):
    return pl.BlockSpec(a.shape, lambda *i: (0,) * len(a.shape))


def near(a):
    return pltpu.with_memory_space_constraint(a, pltpu.VMEM)


def cost(us):
    return pl.CostEstimate(flops=int(us * 1.15e9), bytes_accessed=1024, transcendentals=0)


def lists_kernel(rows, count, inner, forward, at_ref, cols_ref, want_o, slot_o):
    me = at_ref[0]
    cols = cols_ref[...]
    rel = (cols // rows) ^ me
    loc = cols % rows
    slots = jnp.zeros_like(cols)
    for k in range(count):
        hit = rel == k
        least = lambda a: jnp.min(jnp.min(a, axis=2, keepdims=True), axis=1, keepdims=True)
        low = least(jnp.where(hit, loc, rows - 1))
        high = -least(jnp.where(hit, -loc, 0))
        want_o[:, :, 2 * k : 2 * k + 1] = low
        want_o[:, :, 2 * k + 1 : 2 * k + 2] = high
        second = jnp.where(loc == low, 0, 1)
        if forward:
            o = me // inner
            middle = (o == 1) | (o == 2)
            inside = {4: 3 * rows + loc, 5: 7 * rows + second, 6: 2 * rows + loc, 7: 6 * rows + second}
            if k < 4:
                at = {0: loc, 1: 4 * rows + second, 2: rows + loc, 3: 5 * rows + second}[k]
            else:
                at = jnp.where(middle, inside[k], (4 + k) * rows + second)
        elif k < inner:
            at = k * rows + loc
        else:
            at = inner * rows + (k - inner) * 2 + second
        slots = jnp.where(hit, at, slots)
    slot_o[...] = slots


def lists(at, cols, rows, count, inner, forward):
    outs = [
        jax.ShapeDtypeStruct((cols.shape[0], 1, 2 * count), jnp.int32),
        jax.ShapeDtypeStruct(cols.shape, jnp.int32),
    ]
    return pl.pallas_call(
        functools.partial(lists_kernel, rows, count, inner, forward),
        grid_spec=pltpu.PrefetchScalarGridSpec(
            num_scalar_prefetch=1,
            grid=(1,),
            in_specs=[whole(cols)],
            out_specs=[whole(a) for a in outs],
        ),
        out_shape=outs,
        cost_estimate=cost(1),
        name="lists",
    )(at, cols)


def weights_kernel(at_ref, pos_ref, qkv_ref, proj_ref, gain_ref, up_ref, down_ref, space_ref, *refs):
    pos_o, qkv_o, proj_o, gain_o, up_o, down_o, space_o, pos_s = refs
    width = proj_ref.shape[0]
    head_dim = width // HEADS
    snaps = pos_o.shape[0]
    pos_s[...] = pos_ref[...].astype(F32)
    pos_o[...] = pos_s[pl.ds(at_ref[1] * snaps, snaps), :]
    to = lax.broadcasted_iota(jnp.int32, (width, width), 0)
    source = lax.broadcasted_iota(jnp.int32, (width, width), 1)
    by_head = jnp.where((to % HEADS) * head_dim + to // HEADS == source, 1.0, 0.0).astype(BF16)
    for i in range(3):
        part = slice(i * width, (i + 1) * width)
        qkv_o[part, :] = dot_nt(by_head, qkv_ref[:, part]).astype(BF16)
    flip = lambda a: a.astype(F32).T.astype(BF16)
    proj_o[...] = dot_nt(flip(proj_ref[...]), by_head).astype(BF16)
    gain_o[...] = jnp.broadcast_to(gain_ref[...], gain_o.shape).T
    for i in range(up_ref.shape[1] // width):
        part = slice(i * width, (i + 1) * width)
        up_o[part, :] = flip(up_ref[:, part])
        down_o[:, part] = flip(down_ref[part, :])
    space_o[...] = flip(space_ref[...])


def turned(at, snaps, positions, qkv, proj, gain, up, down, space):
    width = proj.shape[0]
    ins = [positions, qkv, proj, gain.reshape(1, width), up, down, space]
    shape = jax.ShapeDtypeStruct
    outs = [
        shape((snaps, width), F32),
        shape((3 * width, width), BF16),
        shape((width, width), BF16),
        shape((width, width), F32),
        shape((up.shape[1], width), BF16),
        shape((width, down.shape[0]), BF16),
        shape((width, width), BF16),
    ]
    return pl.pallas_call(
        weights_kernel,
        grid_spec=pltpu.PrefetchScalarGridSpec(
            num_scalar_prefetch=1,
            grid=(1,),
            in_specs=[whole(a) for a in ins],
            out_specs=[whole(a) for a in outs],
            scratch_shapes=[pltpu.VMEM(positions.shape, F32)],
        ),
        out_shape=outs,
        compiler_params=pltpu.CompilerParams(vmem_limit_bytes=VMEM),
        cost_estimate=cost(2),
        name="turn_weights",
    )(at, *ins)


def pick_kernel(jobs, wants, offsets, *refs):
    outs = refs[len(refs) - len(jobs) :]
    want_refs, srcs = refs[:wants], refs[wants : len(refs) - len(jobs)]
    for (which, pairs, lo, _), out in zip(jobs, outs):
        for s in range(out.shape[0]):
            for j, (src, rel) in enumerate(pairs):
                for i in range(2):
                    block = want_refs[which][lo + s, 0, 2 * rel + i]
                    out[s, 2 * j + i] = srcs[src][lo + s - offsets[src], block]


def pick(srcs, offsets, wants, jobs):
    size, width = srcs[0].shape[2:]
    shapes = [
        jax.ShapeDtypeStruct((hi - lo, 2 * len(pairs), size, width), BF16)
        for _, pairs, lo, hi in jobs
    ]
    return pl.pallas_call(
        functools.partial(pick_kernel, jobs, len(wants), offsets),
        grid_spec=pltpu.PrefetchScalarGridSpec(
            num_scalar_prefetch=len(wants),
            grid=(1,),
            in_specs=[pl.BlockSpec(memory_space=pltpu.VMEM)] * len(srcs),
            out_specs=[whole(a) for a in shapes],
        ),
        out_shape=shapes,
        compiler_params=pltpu.CompilerParams(vmem_limit_bytes=VMEM),
        cost_estimate=cost(1),
        name="pick_blocks",
    )(*wants, *[near(a) for a in srcs])


def spatial_kernel(start, offsets, slot_ref, vals_ref, weight_ref, pos_ref, *refs):
    srcs, (*outs, held, vals, sums, own_sem, vals_sem) = refs[: len(offsets)], refs[len(offsets) :]
    snaps, rows, tiles, size, _ = vals.shape
    each = rows // len(outs)
    span = slice(start - offsets[0], start - offsets[0] + snaps)
    own = pltpu.make_async_copy(srcs[0].at[span], held.at[0], own_sem)
    own.start()
    arriving = []
    for s in range(snaps):
        arriving.append(pltpu.make_async_copy(vals_ref.at[start + s], vals.at[s], vals_sem.at[s]))
        arriving[s].start()
    unit = 1
    for src, offset in zip(srcs[1:], offsets[1:]):
        for first in range(0, src.shape[1], rows):
            n = min(rows, src.shape[1] - first)
            some = src[start - offset : start - offset + snaps, first : first + n]
            held[unit, :, :n] = some
            unit += 1
    own.wait()
    for s in range(snaps):
        arriving[s].wait()
        for r in range(rows):
            left = jnp.concatenate([vals[s, r, k] for k in range(tiles)], axis=1)
            right = []
            for k in range(tiles):
                slot = slot_ref[start + s, r, k]
                right.append(held[slot // rows, s, slot % rows])
            summed = dot(left, jnp.concatenate(right, axis=0)).astype(BF16)
            sums[(s * rows + r) * size : (s * rows + r + 1) * size, :] = summed
    for s in range(snaps):
        pos = pos_ref[start + s : start + s + 1, :]
        position = jnp.broadcast_to(pos, (size, pos.shape[1])).T
        some = sums[s * rows * size : (s + 1) * rows * size, :]
        hidden = jnp.maximum(dot_nt(weight_ref[...], some), 0.0).astype(BF16).astype(F32)
        for r in range(rows):
            mixed = hidden[:, r * size : (r + 1) * size] + position
            outs[r // each][r % each, s] = mixed.astype(BF16)


def spatial(slots, vals, start, stop, weight_t, pos, srcs, parts):
    rows, tiles, size, _ = vals.shape[1:]
    snaps = stop - start
    width = weight_t.shape[0]
    units = sum(-(-a.shape[1] // rows) for a, _ in srcs)
    anywhere = pl.BlockSpec(memory_space=pl.ANY)
    out = jax.ShapeDtypeStruct((rows // parts, snaps, width, size), BF16)
    return pl.pallas_call(
        functools.partial(spatial_kernel, start, [first for _, first in srcs]),
        grid_spec=pltpu.PrefetchScalarGridSpec(
            num_scalar_prefetch=1,
            grid=(1,),
            in_specs=[anywhere, whole(weight_t), whole(pos), anywhere]
            + [pl.BlockSpec(memory_space=pltpu.VMEM)] * (len(srcs) - 1),
            out_specs=[whole(out)] * parts,
            scratch_shapes=[
                pltpu.VMEM((units, snaps, rows, size, width), BF16),
                pltpu.VMEM((snaps, rows, tiles, size, size), BF16),
                pltpu.VMEM((snaps * rows * size, width), BF16),
                pltpu.SemaphoreType.DMA,
                pltpu.SemaphoreType.DMA((snaps,)),
            ],
        ),
        out_shape=[out] * parts,
        compiler_params=pltpu.CompilerParams(vmem_limit_bytes=VMEM),
        cost_estimate=cost(snaps),
        name="spatial",
    )(slots, vals, weight_t, pos, srcs[0][0], *[near(a) for a, _ in srcs[1:]])


def scales(width):
    return 1.0 / (CAP * math.sqrt(width // HEADS)), CAP * math.log2(math.e)


def attend(q_ref, k_ref, v_ref, at, keys, sums):
    width = q_ref.shape[1]
    spans = [slice(d, d + HEADS) for d in range(0, width, HEADS)]
    steep = scales(width)[1]
    q = [q_ref[at, span] for span in spans]
    total, acc = sums if sums else (None, None)
    for u in keys:
        raw = q[0] * k_ref[u, spans[0]]
        for d in range(1, len(spans)):
            raw = raw + q[d] * k_ref[u, spans[d]]
        e = jnp.exp2(steep * jnp.tanh(raw))
        values = [e * v_ref[u, span] for span in spans]
        total = e if total is None else total + e
        acc = values if acc is None else [one + more for one, more in zip(acc, values)]
    return total, acc


def own_kernel(sizes, qkv_ref, *refs):
    arrays = refs[: len(sizes)]
    q_out, acc_out, total_out, q_s, k_s, v_s = refs[len(sizes) :]
    snaps = sum(sizes)
    g = pl.program_id(0)
    width, lanes = arrays[0].shape[2:]
    scale = scales(width)[0]
    found = [a[g, s] for a, n in zip(arrays, sizes) for s in range(n)]
    for first in range(0, snaps, 4):
        some = found[first : first + 4]
        got = dot(qkv_ref[...], jnp.concatenate(some, axis=1)).astype(BF16)
        for j in range(len(some)):
            part = got[:, j * lanes : (j + 1) * lanes]
            q_out[0, first + j] = part[:width]
            q_s[first + j] = part[:width].astype(F32) * scale
            k_s[first + j] = part[width : 2 * width].astype(F32)
            v_s[first + j] = part[2 * width :].astype(F32)
    for s in range(snaps):
        total, acc = attend(q_s, k_s, v_s, s, range(s + 1), None)
        total_out[0, s] = total
        for d, one in enumerate(acc):
            acc_out[0, s, d * HEADS : (d + 1) * HEADS] = one


def own_part(qkv_t, arrays):
    groups, _, width, lanes = arrays[0].shape
    sizes = [a.shape[1] for a in arrays]
    snaps = sum(sizes)
    shape = jax.ShapeDtypeStruct
    outs = [
        shape((groups, snaps, width, lanes), BF16),
        shape((groups, snaps, width, lanes), F32),
        shape((groups, snaps, HEADS, lanes), F32),
    ]
    return pl.pallas_call(
        functools.partial(own_kernel, sizes),
        grid=(groups,),
        in_specs=[whole(qkv_t)] + [pl.BlockSpec(memory_space=pltpu.VMEM)] * len(arrays),
        out_specs=[pl.BlockSpec((1,) + a.shape[1:], lambda g: (g, 0, 0, 0)) for a in outs],
        scratch_shapes=[pltpu.VMEM((snaps, width, lanes), F32)] * 3,
        out_shape=outs,
        compiler_params=pltpu.CompilerParams(vmem_limit_bytes=VMEM),
        cost_estimate=cost(6),
        name="temporal_own",
    )(qkv_t, *[near(a) for a in arrays])


def temporal_kernel(sizes, others, me_ref, qkv_ref, proj_ref, gain_ref, up_ref, down_ref, *refs):
    count = 1 + others
    arrays = refs[: count * len(sizes)]
    q_ref, acc_ref, total_ref, out_ref, k_s, v_s, q_s, acc_s, total_s, att_s = refs[-10:]
    snaps = sum(sizes)
    width, lanes = arrays[0].shape[2:]
    me, g = me_ref[0], pl.program_id(0)
    scale = scales(width)[0]
    spans = [slice(d, d + HEADS) for d in range(0, width, HEADS)]

    def held(i):
        return [arrays[c * count + i][g, s] for c, n in enumerate(sizes) for s in range(n)]

    def project(i):
        base = (me ^ i) * snaps
        found = held(i)
        for first in range(0, snaps, 4):
            some = found[first : first + 4]
            got = dot(qkv_ref[width:, :], jnp.concatenate(some, axis=1)).astype(BF16).astype(F32)
            for j in range(len(some)):
                part = got[:, j * lanes : (j + 1) * lanes]
                k_s[base + first + j] = part[:width]
                v_s[base + first + j] = part[width:]

    for i in range(1, count):
        pl.when((me ^ i) < me)(functools.partial(project, i))
    for at in range(snaps):
        q_s[at] = q_ref[g, at].astype(F32) * scale
        acc_s[at] = acc_ref[g, at]
        total_s[at] = total_ref[g, at]

    def earlier(m, none):
        keys = [m * snaps + j for j in range(snaps)]
        for at in range(snaps):
            sums = total_s[at], [acc_s[at, span] for span in spans]
            total_s[at], acc = attend(q_s, k_s, v_s, at, keys, sums)
            for span, one in zip(spans, acc):
                acc_s[at, span] = one
        return none

    lax.fori_loop(0, me, earlier, 0)

    mine = held(0)
    for at in range(snaps):
        inv = 1.0 / total_s[at]
        for span in spans:
            att_s[span, at * lanes : (at + 1) * lanes] = (acc_s[at, span] * inv).astype(BF16)
    half = snaps // 2
    for h in range(2):
        span = slice(h * half * lanes, (h + 1) * half * lanes)
        base = jnp.concatenate(mine[h * half : (h + 1) * half], axis=1).astype(F32)
        stream = base + dot(proj_ref[...], att_s[:, span])
        centre = jnp.mean(stream, axis=0, keepdims=True)
        away = stream - centre
        spread = jnp.mean(away * away, axis=0, keepdims=True)
        gain = jnp.concatenate([gain_ref[...]] * half, axis=1)
        normed = (away * lax.rsqrt(spread + EPS) * gain).astype(BF16)
        expanded = jnp.maximum(dot(up_ref[...], normed), 0.0).astype(BF16)
        out = stream + dot(down_ref[...], expanded)
        for i in range(half):
            out_ref[h * half + i] = out[:, i * lanes : (i + 1) * lanes].T.astype(BF16)


def temporal(me, weights, chunks, own):
    groups, _, width, lanes = chunks[0][0].shape
    count = len(chunks[0])
    sizes = [chunk[0].shape[1] for chunk in chunks]
    snaps = sum(sizes)
    parts = [a for chunk in chunks for a in chunk] + list(own)
    return pl.pallas_call(
        functools.partial(temporal_kernel, sizes, count - 1),
        grid_spec=pltpu.PrefetchScalarGridSpec(
            num_scalar_prefetch=1,
            grid=(groups,),
            in_specs=[whole(a) for a in weights]
            + [pl.BlockSpec(memory_space=pltpu.VMEM)] * len(parts),
            out_specs=pl.BlockSpec((snaps, lanes, width), lambda g, i: (0, g, 0)),
            scratch_shapes=[
                pltpu.VMEM((snaps * count, width, lanes), F32),
                pltpu.VMEM((snaps * count, width, lanes), F32),
                pltpu.VMEM((snaps, width, lanes), F32),
                pltpu.VMEM((snaps, width, lanes), F32),
                pltpu.VMEM((snaps, HEADS, lanes), F32),
                pltpu.VMEM((width, snaps * lanes), BF16),
            ],
        ),
        out_shape=jax.ShapeDtypeStruct((snaps, groups * lanes, width), BF16),
        compiler_params=pltpu.CompilerParams(vmem_limit_bytes=VMEM),
        cost_estimate=cost(10),
        name="temporal",
    )(me, *weights, *[near(a) for a in parts])


def send(a, k):
    return lax.ppermute(a, "vert", [(v, v ^ k) for v in range(lax.axis_size("vert"))])


def exchange_direct(blocks, want, inner):
    snaps = blocks.shape[0]
    count = lax.axis_size("vert")
    outer = count // inner
    wants = [send(want, k * inner) for k in range(1, outer)]
    layer = [blocks] + [send(blocks, j) for j in range(1, inner)]
    jobs = [
        (k - 1, [(j, k * inner + j) for j in range(inner)], 0, snaps) for k in range(1, outer)
    ]
    picked = pick(layer, [0] * inner, wants, jobs)
    arrived = [send(picked[k - 1], k * inner) for k in range(1, outer)]
    return [(0, snaps, lambda before: [(a, 0) for a in layer + arrived])]


def exchange_forward(blocks, want, turned_weights):
    snaps = blocks.shape[0]
    layers = lambda pairs, x=0: [(a * 2 + i, b * 2 + (i ^ x)) for a, b in pairs for i in range(2)]
    go = lambda a, pairs, x=0: lax.ppermute(a, "vert", layers(pairs, x))
    cross = [(1, 2), (2, 1)]
    ends = [(2, 3), (1, 0)]
    back = [(3, 2), (0, 1)]
    inside = [(1, 1), (2, 2)]

    p1, beside = go(blocks, cross), send(blocks, 2)
    wants = [send(want, 1), None, None]
    (xo,) = pick([blocks], [0], wants[:1], [(0, [(0, 1)], 0, snaps)])
    xo = send(xo, 1)
    both = go(jnp.concatenate([want, wants[0]], axis=1), back)
    beside, both, xo, p1, turned_weights = after((beside, both, xo, p1, turned_weights))
    wants[1:] = both[:, :1], both[:, 1:]

    p2 = go(beside, cross)
    jobs = [(1, [(0, 4)], 0, snaps), (2, [(0, 5)], 0, snaps), (0, [(0, 7)], 0, snaps)]
    f0, f1, x1, xn = pick([p1, beside], [0, 0], wants, jobs + [(0, [(1, 3)], 0, snaps)])
    f0, f1, x1, xn = go(f0, ends), go(f1, ends, 1), go(x1, inside, 1), send(xn, 1)

    cuts = sorted({0, snaps // 4, -(-5 * snaps // 8), snaps})
    spans = list(zip(cuts, cuts[1:]))
    jobs = [(0, [(0, 5)], 0, snaps)]
    for span in spans:
        jobs += [(1, [(0, 6)], *span), (2, [(0, 7)], *span)]
    x2, *late = pick([p2], [0], wants, jobs)
    x2 = go(x2, inside, 1)
    all_snaps = [(a, 0) for a in (blocks, beside, p1, p2, xo, xn, x1, x2, f0, f1)]

    def part(span, a, b):
        def get(before):
            pair = (a, b) if before is None else after((a, b, before))[:2]
            sent = go(pair[0], ends), go(pair[1], ends, 1)
            return all_snaps + [(c, span[0]) for c in sent]

        return (*span, get)

    return [part(span, a, b) for span, a, b in zip(spans, late[::2], late[1::2])], turned_weights


def gather_times(own):
    times = lax.axis_size("tm")
    got = [own] + [None] * (times - 1)
    for k in range(1, times):
        if k == 1 or k % 2 == 0:
            pairs = [(m, m ^ k) for m in range(times) if m < (m ^ k)]
            got[k] = lax.ppermute(own, "tm", pairs)
    return got


def pass_on(got, late):
    times = lax.axis_size("tm")
    got = list(got)
    for k in range(3, times, 2):
        pairs = [(m, m ^ 1) for m in range(times) if (m ^ (k - 1)) < m]
        got[k - 1], _ = after((got[k - 1], late))
        got[k] = lax.ppermute(got[k - 1], "tm", pairs)
    return got


def local(
    features,
    tile_cols,
    tile_vals,
    space_weight,
    positions,
    attn_proj,
    attn_out,
    norm_gain,
    mlp_up,
    mlp_down,
):
    snaps, verts, width = features.shape
    rows, tiles, size = tile_vals.shape[1:4]
    count = lax.axis_size("vert")
    outer, inner = split_axis(count)
    me_t = lax.axis_index("tm").astype(jnp.int32)
    me_v = lax.axis_index("vert").astype(jnp.int32)
    blocks = features.reshape(snaps, rows, size, width)

    forward = (outer, inner) == (4, 2)
    at = jnp.stack([me_v, me_t])
    want, slots = lists(at, tile_cols, rows, count, inner, forward)
    pos, *weights, space_t = turned(
        at, snaps, positions, attn_proj, attn_out, norm_gain, mlp_up, mlp_down, space_weight
    )
    me = me_t.reshape(1)
    if forward:
        parts, space_t = exchange_forward(blocks, want, space_t)
    else:
        parts = exchange_direct(blocks, want, inner)

    started, owns = [], []
    held = [get(None) for _, _, get in parts[:2]]
    for c, (start, stop, get) in enumerate(parts):
        srcs = held[c] if c < 2 else get(owns[c - 2])
        if owns:
            sent = [a for a in started[c - 2] if a is not None] if c > 1 else []
            srcs = [(after((srcs[0][0], owns[-1], *sent))[0], srcs[0][1])] + srcs[1:]
        owns.append(spatial(slots, tile_vals, start, stop, space_t, pos, srcs, 1)[0])
        started.append(gather_times(owns[-1]))
    chunks = [pass_on(got, own) for got, own in zip(started, owns[1:] + owns[-1:])]
    return temporal(me, weights, chunks, own_part(weights[0], owns))


def solution(mesh):
    placed = (
        P("tm", "vert", None),
        P("tm", "vert", None),
        P("tm", "vert", None, None, None),
        P(),
        P(),
        P(),
        P(),
        P(),
        P(),
        P(),
    )
    return jax.shard_map(
        local, mesh=mesh, in_specs=placed, out_specs=P("tm", "vert", None), check_vma=False
    )
```

```python
import functools
import math

import jax
import jax.numpy as jnp
from jax import lax
from jax.experimental import pallas as pl
from jax.experimental.pallas import tpu as pltpu
from jax.sharding import PartitionSpec as P

HEADS = 16
CAP = 4.0
EPS = 1e-05
VMEM = 24 * 1024 * 1024
BF16 = jnp.bfloat16
F32 = jnp.float32
after = lax.optimization_barrier


def split_axis(count):
    inner = 1
    while (inner * 2) * (inner * 2) <= count and count % (inner * 2) == 0:
        inner *= 2
    return count // inner, inner


def dot(a, b):
    return jnp.dot(a, b, preferred_element_type=F32)


def dot_nt(a, b):
    return lax.dot_general(a, b, (((1,), (1,)), ((), ())), preferred_element_type=F32)


def whole(a):
    return pl.BlockSpec(a.shape, lambda *i: (0,) * len(a.shape))


def near(a):
    return pltpu.with_memory_space_constraint(a, pltpu.VMEM)


def cost(us):
    return pl.CostEstimate(flops=int(us * 1.15e9), bytes_accessed=1024, transcendentals=0)


def lists_kernel(rows, count, inner, forward, at_ref, cols_ref, want_o, slot_o):
    me = at_ref[0]
    cols = cols_ref[...]
    rel = (cols // rows) ^ me
    loc = cols % rows
    slots = jnp.zeros_like(cols)
    for k in range(count):
        hit = rel == k
        least = lambda a: jnp.min(jnp.min(a, axis=2, keepdims=True), axis=1, keepdims=True)
        low = least(jnp.where(hit, loc, rows - 1))
        high = -least(jnp.where(hit, -loc, 0))
        want_o[:, :, 2 * k : 2 * k + 1] = low
        want_o[:, :, 2 * k + 1 : 2 * k + 2] = high
        second = jnp.where(loc == low, 0, 1)
        if forward:
            o = me // inner
            middle = (o == 1) | (o == 2)
            inside = {4: 3 * rows + loc, 5: 7 * rows + second, 6: 2 * rows + loc, 7: 6 * rows + second}
            if k < 4:
                at = {0: loc, 1: 4 * rows + second, 2: rows + loc, 3: 5 * rows + second}[k]
            else:
                at = jnp.where(middle, inside[k], (4 + k) * rows + second)
        elif k < inner:
            at = k * rows + loc
        else:
            at = inner * rows + (k - inner) * 2 + second
        slots = jnp.where(hit, at, slots)
    slot_o[...] = slots


def lists(at, cols, rows, count, inner, forward):
    outs = [
        jax.ShapeDtypeStruct((cols.shape[0], 1, 2 * count), jnp.int32),
        jax.ShapeDtypeStruct(cols.shape, jnp.int32),
    ]
    return pl.pallas_call(
        functools.partial(lists_kernel, rows, count, inner, forward),
        grid_spec=pltpu.PrefetchScalarGridSpec(
            num_scalar_prefetch=1,
            grid=(1,),
            in_specs=[whole(cols)],
            out_specs=[whole(a) for a in outs],
        ),
        out_shape=outs,
        cost_estimate=cost(1),
        name="lists",
    )(at, cols)


def weights_kernel(at_ref, pos_ref, qkv_ref, proj_ref, gain_ref, up_ref, down_ref, space_ref, *refs):
    pos_o, qkv_o, proj_o, gain_o, up_o, down_o, space_o, pos_s = refs
    width = proj_ref.shape[0]
    head_dim = width // HEADS
    snaps = pos_o.shape[0]
    pos_s[...] = pos_ref[...].astype(F32)
    pos_o[...] = pos_s[pl.ds(at_ref[1] * snaps, snaps), :]
    to = lax.broadcasted_iota(jnp.int32, (width, width), 0)
    source = lax.broadcasted_iota(jnp.int32, (width, width), 1)
    by_head = jnp.where((to % HEADS) * head_dim + to // HEADS == source, 1.0, 0.0).astype(BF16)
    for i in range(3):
        part = slice(i * width, (i + 1) * width)
        qkv_o[part, :] = dot_nt(by_head, qkv_ref[:, part]).astype(BF16)
    flip = lambda a: a.astype(F32).T.astype(BF16)
    proj_o[...] = dot_nt(flip(proj_ref[...]), by_head).astype(BF16)
    gain_o[...] = jnp.broadcast_to(gain_ref[...], gain_o.shape).T
    for i in range(up_ref.shape[1] // width):
        part = slice(i * width, (i + 1) * width)
        up_o[part, :] = flip(up_ref[:, part])
        down_o[:, part] = flip(down_ref[part, :])
    space_o[...] = flip(space_ref[...])


def turned(at, snaps, positions, qkv, proj, gain, up, down, space):
    width = proj.shape[0]
    ins = [positions, qkv, proj, gain.reshape(1, width), up, down, space]
    shape = jax.ShapeDtypeStruct
    outs = [
        shape((snaps, width), F32),
        shape((3 * width, width), BF16),
        shape((width, width), BF16),
        shape((width, width), F32),
        shape((up.shape[1], width), BF16),
        shape((width, down.shape[0]), BF16),
        shape((width, width), BF16),
    ]
    return pl.pallas_call(
        weights_kernel,
        grid_spec=pltpu.PrefetchScalarGridSpec(
            num_scalar_prefetch=1,
            grid=(1,),
            in_specs=[whole(a) for a in ins],
            out_specs=[whole(a) for a in outs],
            scratch_shapes=[pltpu.VMEM(positions.shape, F32)],
        ),
        out_shape=outs,
        compiler_params=pltpu.CompilerParams(vmem_limit_bytes=VMEM),
        cost_estimate=cost(2),
        name="turn_weights",
    )(at, *ins)


def pick_kernel(jobs, wants, offsets, *refs):
    outs = refs[len(refs) - len(jobs) :]
    want_refs, srcs = refs[:wants], refs[wants : len(refs) - len(jobs)]
    for (which, pairs, lo, _), out in zip(jobs, outs):
        for s in range(out.shape[0]):
            for j, (src, rel) in enumerate(pairs):
                for i in range(2):
                    block = want_refs[which][lo + s, 0, 2 * rel + i]
                    out[s, 2 * j + i] = srcs[src][lo + s - offsets[src], block]


def pick(srcs, offsets, wants, jobs):
    size, width = srcs[0].shape[2:]
    shapes = [
        jax.ShapeDtypeStruct((hi - lo, 2 * len(pairs), size, width), BF16)
        for _, pairs, lo, hi in jobs
    ]
    return pl.pallas_call(
        functools.partial(pick_kernel, jobs, len(wants), offsets),
        grid_spec=pltpu.PrefetchScalarGridSpec(
            num_scalar_prefetch=len(wants),
            grid=(1,),
            in_specs=[pl.BlockSpec(memory_space=pltpu.VMEM)] * len(srcs),
            out_specs=[whole(a) for a in shapes],
        ),
        out_shape=shapes,
        compiler_params=pltpu.CompilerParams(vmem_limit_bytes=VMEM),
        cost_estimate=cost(1),
        name="pick_blocks",
    )(*wants, *[near(a) for a in srcs])


def spatial_kernel(start, offsets, slot_ref, vals_ref, weight_ref, pos_ref, *refs):
    srcs, (*outs, held, vals, sums, own_sem, vals_sem) = refs[: len(offsets)], refs[len(offsets) :]
    snaps, rows, tiles, size, _ = vals.shape
    each = rows // len(outs)
    span = slice(start - offsets[0], start - offsets[0] + snaps)
    own = pltpu.make_async_copy(srcs[0].at[span], held.at[0], own_sem)
    own.start()
    arriving = []
    for s in range(snaps):
        arriving.append(pltpu.make_async_copy(vals_ref.at[start + s], vals.at[s], vals_sem.at[s]))
        arriving[s].start()
    unit = 1
    for src, offset in zip(srcs[1:], offsets[1:]):
        for first in range(0, src.shape[1], rows):
            n = min(rows, src.shape[1] - first)
            some = src[start - offset : start - offset + snaps, first : first + n]
            held[unit, :, :n] = some
            unit += 1
    own.wait()
    for s in range(snaps):
        arriving[s].wait()
        for r in range(rows):
            left = jnp.concatenate([vals[s, r, k] for k in range(tiles)], axis=1)
            right = []
            for k in range(tiles):
                slot = slot_ref[start + s, r, k]
                right.append(held[slot // rows, s, slot % rows])
            summed = dot(left, jnp.concatenate(right, axis=0)).astype(BF16)
            sums[(s * rows + r) * size : (s * rows + r + 1) * size, :] = summed
    for s in range(snaps):
        pos = pos_ref[start + s : start + s + 1, :]
        position = jnp.broadcast_to(pos, (size, pos.shape[1])).T
        some = sums[s * rows * size : (s + 1) * rows * size, :]
        hidden = jnp.maximum(dot_nt(weight_ref[...], some), 0.0).astype(BF16).astype(F32)
        for r in range(rows):
            mixed = hidden[:, r * size : (r + 1) * size] + position
            outs[r // each][r % each, s] = mixed.astype(BF16)


def spatial(slots, vals, start, stop, weight_t, pos, srcs, parts):
    rows, tiles, size, _ = vals.shape[1:]
    snaps = stop - start
    width = weight_t.shape[0]
    units = sum(-(-a.shape[1] // rows) for a, _ in srcs)
    anywhere = pl.BlockSpec(memory_space=pl.ANY)
    out = jax.ShapeDtypeStruct((rows // parts, snaps, width, size), BF16)
    return pl.pallas_call(
        functools.partial(spatial_kernel, start, [first for _, first in srcs]),
        grid_spec=pltpu.PrefetchScalarGridSpec(
            num_scalar_prefetch=1,
            grid=(1,),
            in_specs=[anywhere, whole(weight_t), whole(pos), anywhere]
            + [pl.BlockSpec(memory_space=pltpu.VMEM)] * (len(srcs) - 1),
            out_specs=[whole(out)] * parts,
            scratch_shapes=[
                pltpu.VMEM((units, snaps, rows, size, width), BF16),
                pltpu.VMEM((snaps, rows, tiles, size, size), BF16),
                pltpu.VMEM((snaps * rows * size, width), BF16),
                pltpu.SemaphoreType.DMA,
                pltpu.SemaphoreType.DMA((snaps,)),
            ],
        ),
        out_shape=[out] * parts,
        compiler_params=pltpu.CompilerParams(vmem_limit_bytes=VMEM),
        cost_estimate=cost(snaps),
        name="spatial",
    )(slots, vals, weight_t, pos, srcs[0][0], *[near(a) for a, _ in srcs[1:]])


def scales(width):
    return 1.0 / (CAP * math.sqrt(width // HEADS)), CAP * math.log2(math.e)


def attend(q_ref, k_ref, v_ref, at, keys, sums):
    width = q_ref.shape[1]
    spans = [slice(d, d + HEADS) for d in range(0, width, HEADS)]
    steep = scales(width)[1]
    q = [q_ref[at, span] for span in spans]
    scale = scales(width)[0]
    total, acc = sums if sums else (None, None)
    for u in keys:
        raw = q[0] * k_ref[u, spans[0]]
        for d in range(1, len(spans)):
            raw = raw + q[d] * k_ref[u, spans[d]]
        e = jnp.exp2(steep * jnp.tanh(raw.astype(F32) * scale))
        values = [e * v_ref[u, span] for span in spans]
        total = e if total is None else total + e
        acc = values if acc is None else [one + more for one, more in zip(acc, values)]
    return total, acc


def own_kernel(sizes, qkv_ref, *refs):
    arrays = refs[: len(sizes)]
    q_out, acc_out, total_out, q_s, k_s, v_s = refs[len(sizes) :]
    snaps = sum(sizes)
    g = pl.program_id(0)
    width, lanes = arrays[0].shape[2:]
    found = [a[g, s] for a, n in zip(arrays, sizes) for s in range(n)]
    for first in range(0, snaps, 4):
        some = found[first : first + 4]
        got = dot(qkv_ref[...], jnp.concatenate(some, axis=1)).astype(BF16)
        for j in range(len(some)):
            part = got[:, j * lanes : (j + 1) * lanes]
            q_out[0, first + j] = part[:width]
            q_s[first + j] = part[:width]
            k_s[first + j] = part[width : 2 * width]
            v_s[first + j] = part[2 * width :].astype(F32)
    for s in range(snaps):
        total, acc = attend(q_s, k_s, v_s, s, range(s + 1), None)
        total_out[0, s] = total
        for d, one in enumerate(acc):
            acc_out[0, s, d * HEADS : (d + 1) * HEADS] = one


def own_part(qkv_t, arrays):
    groups, _, width, lanes = arrays[0].shape
    sizes = [a.shape[1] for a in arrays]
    snaps = sum(sizes)
    shape = jax.ShapeDtypeStruct
    outs = [
        shape((groups, snaps, width, lanes), BF16),
        shape((groups, snaps, width, lanes), F32),
        shape((groups, snaps, HEADS, lanes), F32),
    ]
    return pl.pallas_call(
        functools.partial(own_kernel, sizes),
        grid=(groups,),
        in_specs=[whole(qkv_t)] + [pl.BlockSpec(memory_space=pltpu.VMEM)] * len(arrays),
        out_specs=[pl.BlockSpec((1,) + a.shape[1:], lambda g: (g, 0, 0, 0)) for a in outs],
        scratch_shapes=[pltpu.VMEM((snaps, width, lanes), t) for t in (BF16, BF16, F32)],
        out_shape=outs,
        compiler_params=pltpu.CompilerParams(vmem_limit_bytes=VMEM),
        cost_estimate=cost(6),
        name="temporal_own",
    )(qkv_t, *[near(a) for a in arrays])


def temporal_kernel(sizes, others, me_ref, qkv_ref, proj_ref, gain_ref, up_ref, down_ref, *refs):
    count = 1 + others
    arrays = refs[: count * len(sizes)]
    q_ref, acc_ref, total_ref, out_ref, k_s, v_s, q_s, acc_s, total_s, att_s = refs[-10:]
    snaps = sum(sizes)
    width, lanes = arrays[0].shape[2:]
    me, g = me_ref[0], pl.program_id(0)
    spans = [slice(d, d + HEADS) for d in range(0, width, HEADS)]

    def held(i):
        return [arrays[c * count + i][g, s] for c, n in enumerate(sizes) for s in range(n)]

    def project(i):
        base = (me ^ i) * snaps
        found = held(i)
        for first in range(0, snaps, 4):
            some = found[first : first + 4]
            got = dot(qkv_ref[width:, :], jnp.concatenate(some, axis=1)).astype(BF16).astype(F32)
            for j in range(len(some)):
                part = got[:, j * lanes : (j + 1) * lanes]
                k_s[base + first + j] = part[:width].astype(BF16)
                v_s[base + first + j] = part[width:]

    for i in range(1, count):
        pl.when((me ^ i) < me)(functools.partial(project, i))
    for at in range(snaps):
        q_s[at] = q_ref[g, at]
        acc_s[at] = acc_ref[g, at]
        total_s[at] = total_ref[g, at]

    def earlier(m, none):
        keys = [m * snaps + j for j in range(snaps)]
        for at in range(snaps):
            sums = total_s[at], [acc_s[at, span] for span in spans]
            total_s[at], acc = attend(q_s, k_s, v_s, at, keys, sums)
            for span, one in zip(spans, acc):
                acc_s[at, span] = one
        return none

    lax.fori_loop(0, me, earlier, 0)

    mine = held(0)
    for at in range(snaps):
        inv = 1.0 / total_s[at]
        for span in spans:
            att_s[span, at * lanes : (at + 1) * lanes] = (acc_s[at, span] * inv).astype(BF16)
    half = snaps // 2
    for h in range(2):
        span = slice(h * half * lanes, (h + 1) * half * lanes)
        base = jnp.concatenate(mine[h * half : (h + 1) * half], axis=1).astype(F32)
        stream = base + dot(proj_ref[...], att_s[:, span])
        centre = jnp.mean(stream, axis=0, keepdims=True)
        away = stream - centre
        spread = jnp.mean(away * away, axis=0, keepdims=True)
        gain = jnp.concatenate([gain_ref[...]] * half, axis=1)
        normed = (away * lax.rsqrt(spread + EPS) * gain).astype(BF16)
        expanded = jnp.maximum(dot(up_ref[...], normed), 0.0).astype(BF16)
        out = stream + dot(down_ref[...], expanded)
        for i in range(half):
            out_ref[h * half + i] = out[:, i * lanes : (i + 1) * lanes].T.astype(BF16)


def temporal(me, weights, chunks, own):
    groups, _, width, lanes = chunks[0][0].shape
    count = len(chunks[0])
    sizes = [chunk[0].shape[1] for chunk in chunks]
    snaps = sum(sizes)
    parts = [a for chunk in chunks for a in chunk] + list(own)
    return pl.pallas_call(
        functools.partial(temporal_kernel, sizes, count - 1),
        grid_spec=pltpu.PrefetchScalarGridSpec(
            num_scalar_prefetch=1,
            grid=(groups,),
            in_specs=[whole(a) for a in weights]
            + [pl.BlockSpec(memory_space=pltpu.VMEM)] * len(parts),
            out_specs=pl.BlockSpec((snaps, lanes, width), lambda g, i: (0, g, 0)),
            scratch_shapes=[
                pltpu.VMEM((snaps * count, width, lanes), BF16),
                pltpu.VMEM((snaps * count, width, lanes), F32),
                pltpu.VMEM((snaps, width, lanes), BF16),
                pltpu.VMEM((snaps, width, lanes), F32),
                pltpu.VMEM((snaps, HEADS, lanes), F32),
                pltpu.VMEM((width, snaps * lanes), BF16),
            ],
        ),
        out_shape=jax.ShapeDtypeStruct((snaps, groups * lanes, width), BF16),
        compiler_params=pltpu.CompilerParams(vmem_limit_bytes=VMEM),
        cost_estimate=cost(10),
        name="temporal",
    )(me, *weights, *[near(a) for a in parts])


def send(a, k):
    return lax.ppermute(a, "vert", [(v, v ^ k) for v in range(lax.axis_size("vert"))])


def exchange_direct(blocks, want, inner):
    snaps = blocks.shape[0]
    count = lax.axis_size("vert")
    outer = count // inner
    wants = [send(want, k * inner) for k in range(1, outer)]
    layer = [blocks] + [send(blocks, j) for j in range(1, inner)]
    jobs = [
        (k - 1, [(j, k * inner + j) for j in range(inner)], 0, snaps) for k in range(1, outer)
    ]
    picked = pick(layer, [0] * inner, wants, jobs)
    arrived = [send(picked[k - 1], k * inner) for k in range(1, outer)]
    return [(0, snaps, lambda before: [(a, 0) for a in layer + arrived])]


def exchange_forward(blocks, want):
    snaps = blocks.shape[0]
    layers = lambda pairs, x=0: [(a * 2 + i, b * 2 + (i ^ x)) for a, b in pairs for i in range(2)]
    go = lambda a, pairs, x=0: lax.ppermute(a, "vert", layers(pairs, x))
    cross = [(1, 2), (2, 1)]
    ends = [(2, 3), (1, 0)]
    back = [(3, 2), (0, 1)]
    inside = [(1, 1), (2, 2)]

    p1, beside = go(blocks, cross), send(blocks, 2)
    wants = [send(want, 1), None, None]
    (xo,) = pick([blocks], [0], wants[:1], [(0, [(0, 1)], 0, snaps)])
    xo = send(xo, 1)
    both = go(jnp.concatenate([want, wants[0]], axis=1), back)
    beside, both, xo, p1 = after((beside, both, xo, p1))
    wants[1:] = both[:, :1], both[:, 1:]

    p2 = go(beside, cross)
    jobs = [(1, [(0, 4)], 0, snaps), (2, [(0, 5)], 0, snaps), (0, [(0, 7)], 0, snaps)]
    f0, f1, x1, xn = pick([p1, beside], [0, 0], wants, jobs + [(0, [(1, 3)], 0, snaps)])
    f0, f1, x1, xn = go(f0, ends), go(f1, ends, 1), go(x1, inside, 1), send(xn, 1)

    cuts = sorted({0, snaps // 4, -(-5 * snaps // 8), snaps})
    spans = list(zip(cuts, cuts[1:]))
    jobs = [(0, [(0, 5)], 0, snaps)]
    for span in spans:
        jobs += [(1, [(0, 6)], *span), (2, [(0, 7)], *span)]
    x2, *late = pick([p2], [0], wants, jobs)
    x2 = go(x2, inside, 1)
    all_snaps = [(a, 0) for a in (blocks, beside, p1, p2, xo, xn, x1, x2, f0, f1)]

    def part(span, a, b):
        def get(before):
            pair = (a, b) if before is None else after((a, b, before))[:2]
            sent = go(pair[0], ends), go(pair[1], ends, 1)
            return all_snaps + [(c, span[0]) for c in sent]

        return (*span, get)

    return [part(span, a, b) for span, a, b in zip(spans, late[::2], late[1::2])]


def gather_times(own):
    times = lax.axis_size("tm")
    got = [own] + [None] * (times - 1)
    for k in range(1, times):
        if k == 1 or k % 2 == 0:
            pairs = [(m, m ^ k) for m in range(times) if m < (m ^ k)]
            got[k] = lax.ppermute(own, "tm", pairs)
    return got


def pass_on(got, late):
    times = lax.axis_size("tm")
    got = list(got)
    for k in range(3, times, 2):
        pairs = [(m, m ^ 1) for m in range(times) if (m ^ (k - 1)) < m]
        got[k - 1], _ = after((got[k - 1], late))
        got[k] = lax.ppermute(got[k - 1], "tm", pairs)
    return got


def local(
    features,
    tile_cols,
    tile_vals,
    space_weight,
    positions,
    attn_proj,
    attn_out,
    norm_gain,
    mlp_up,
    mlp_down,
):
    snaps, verts, width = features.shape
    rows, tiles, size = tile_vals.shape[1:4]
    count = lax.axis_size("vert")
    outer, inner = split_axis(count)
    me_t = lax.axis_index("tm").astype(jnp.int32)
    me_v = lax.axis_index("vert").astype(jnp.int32)
    blocks = features.reshape(snaps, rows, size, width)

    forward = (outer, inner) == (4, 2)
    at = jnp.stack([me_v, me_t])
    want, slots = lists(at, tile_cols, rows, count, inner, forward)
    pos, *weights, space_t = turned(
        at, snaps, positions, attn_proj, attn_out, norm_gain, mlp_up, mlp_down, space_weight
    )
    me = me_t.reshape(1)
    parts = exchange_forward(blocks, want) if forward else exchange_direct(blocks, want, inner)

    started, owns = [], []
    held = [get(None) for _, _, get in parts[:2]]
    for c, (start, stop, get) in enumerate(parts):
        srcs = held[c] if c < 2 else get(owns[c - 2])
        if owns:
            sent = [a for a in started[c - 2] if a is not None] if c > 1 else []
            srcs = [(after((srcs[0][0], owns[-1], *sent))[0], srcs[0][1])] + srcs[1:]
        owns.append(spatial(slots, tile_vals, start, stop, space_t, pos, srcs, 1)[0])
        started.append(gather_times(owns[-1]))
    chunks = [pass_on(got, own) for got, own in zip(started, owns[1:] + owns[-1:])]
    return temporal(me, weights, chunks, own_part(weights[0], owns))


def solution(mesh):
    placed = (
        P("tm", "vert", None),
        P("tm", "vert", None),
        P("tm", "vert", None, None, None),
        P(),
        P(),
        P(),
        P(),
        P(),
        P(),
        P(),
    )
    return jax.shard_map(
        local, mesh=mesh, in_specs=placed, out_specs=P("tm", "vert", None), check_vma=False
    )
```
